256 devices in a mesh: prompt: 2 (over core), resp: 32 (over z_lo, y, x), head: 4 (over z_hi).
Axes of the slice: x: 4, y: 4, z: 8 (z_hi: 4, z_lo: 2; z = z_hi * 2 + z_lo), core: 2. Of those that a mesh axis runs over, the one named last changes fastest.
Arguments:
- prefix_hidden: bfloat16 [4096, 5120], P(('prompt', 'resp', 'head')), may hold values from -24 to 24
- w_key: bfloat16 [5120, 1024], P(None, 'head'), may hold values from -0.083496094 to 0.083496094
- w_value: bfloat16 [5120, 1024], P(None, 'head'), may hold values from -0.16699219 to 0.16699219
- queries: bfloat16 [128, 256, 5120], P(('prompt', 'resp'), None, 'head'), may hold values from -6 to 6
- resp_keys: bfloat16 [128, 256, 1024], P(('prompt', 'resp'), None, 'head'), may hold values from -6 to 6
- resp_values: bfloat16 [128, 256, 1024], P(('prompt', 'resp'), None, 'head'), may hold values from -15 to 15
- lengths: int32 [128], P(('prompt', 'resp')), may hold values from 1 to 256, as said below
- assign: int32 [128], P(('prompt', 'resp')), may hold values from 0 to 1, as said below
- grad_out: bfloat16 [128, 256, 5120], P(('prompt', 'resp'), None, 'head'), may hold values from -6 to 6
Outputs:
- attn_out: bfloat16 [128, 256, 5120], P(('prompt', 'resp'), None, 'head')
- grad_query: bfloat16 [128, 256, 5120], P(('prompt', 'resp'), None, 'head')
- grad_rkey: bfloat16 [128, 256, 1024], P(('prompt', 'resp'), None, 'head')
- grad_rvalue: bfloat16 [128, 256, 1024], P(('prompt', 'resp'), None, 'head')
- grad_wkey: float32 [5120, 1024], P(('prompt', 'resp'), 'head')
- grad_wvalue: float32 [5120, 1024], P(('prompt', 'resp'), 'head')
The draws below stay inside these ranges and needn't reach their ends.
Inputs may be any that keep to these rules, and one draw needn't show every extreme that they name: Response r's live positions are 0 to lengths[r] - 1; some response has all 256. `assign`: in each block of 64 consecutive responses (one prompt group) every prompt number is named by exactly 32 responses.
All inputs are finite; a program needn't handle non-finite values.
Results may differ from the reference program's by a relative error of at most 0.033.
Values may be sent and summed in bfloat16 or wider, within the bound.
A program may use at most 128 MiB of HBM per device.

```python
import math
import jax
import jax.numpy as jnp
from jax import lax

D = 5120
QH = 40
KVH = 8
HD = 128
RLEN = 256
PLEN = 1024
PROM_GRP = 2
RESP_DEV = 2
GRP = 5
RESP_GRP = 64
PROMPTS = 4
RESPS = 128
N_RESP = 32


def draw_resp_keys(key, part):
    key = jax.random.fold_in(key, 5)
    drawn_base = 1.5 * jax.random.truncated_normal(key, -4.0, 4.0, (RESPS, RLEN, KVH * HD), jnp.float32)
    return drawn_base.astype(jnp.bfloat16)


def draw_queries(key, part):
    key = jax.random.fold_in(key, 6)
    drawn_base = 1.5 * jax.random.truncated_normal(key, -4.0, 4.0, (RESPS, RLEN, QH * HD), jnp.float32)
    return drawn_base.astype(jnp.bfloat16)


def draw_lengths(key, part):
    key = jax.random.fold_in(key, 7)
    drawn = jax.random.randint(key, (RESPS,), 1, RLEN + 1)
    chosen_spot = jax.random.randint(jax.random.fold_in(key, 1), (), 0, RESPS)
    return drawn.at[chosen_spot].set(RLEN).astype(jnp.int32)


def draw_assign(key, part):
    key = jax.random.fold_in(key, 8)

    def per_group(group_index):
        shuffled = jax.random.permutation(jax.random.fold_in(key, group_index), RESP_GRP)
        return shuffled // (RESP_GRP // PROM_GRP)
    groups_count = RESPS // RESP_GRP
    return jax.vmap(per_group)(jnp.arange(groups_count)).reshape(RESPS).astype(jnp.int32)


def with_spikes(values, key, source, target, shards_of, factor):
    def block_of(dim):
        return (jnp.arange(values.shape[dim]) // (values.shape[dim] // shards_of)).reshape((-1,) + (1,) * (values.ndim - 1 - dim))

    first = jax.random.permutation(key, shards_of)[block_of(target)]
    other_side = (block_of(target) + shards_of // 2) % shards_of
    return jnp.where((block_of(source) == first) | (block_of(source) == other_side), factor * values, values)


def block_scale(stream_key, extent, cuts, low, top_value):
    level, own = 1.0, jax.random.fold_in(stream_key, 6)
    for axis_at, shards_of in cuts:
        steps = jnp.exp(jax.random.uniform(jax.random.fold_in(own, axis_at), (shards_of,), jnp.float32, low / len(cuts), top_value / len(cuts)))
        level = level * jnp.repeat(steps, extent[axis_at] // shards_of).reshape([-1 if axis == axis_at else 1 for axis in range(len(extent))])
    return level


def gaussian(key, extent, deviation, limit, pieces=(), kind=jnp.bfloat16):
    entries = deviation * jax.random.normal(key, extent, jnp.float32)
    if pieces:
        entries = entries * block_scale(key, extent, pieces, -0.22, 0.18)
    return jnp.clip(entries, -limit, limit).astype(kind)


def noise_with(rng, shape, scale, bound, cuts, heavy, kind=jnp.bfloat16):
    values = scale * jax.random.normal(rng, shape, jnp.float32)
    if cuts:
        values = values * block_scale(rng, shape, cuts, -0.22, 0.18)
    return jnp.clip(with_spikes(values, jax.random.fold_in(rng, 3), *heavy), -bound, bound).astype(kind)


def setup_inputs(seed: int = 0) -> dict:
    key_of = jax.random.split(jax.random.key(seed), 10)
    return {
        "prefix_hidden": noise_with(key_of[0], (PROMPTS * PLEN, D), 1.0, 24.0, ((0, 256),), (0, 1, 256, 6.0)),
        "w_key": gaussian(key_of[1], (D, KVH * HD), (1.5 / D ** 0.5), 0.083496094, ((1, 4),)),
        "w_value": gaussian(key_of[2], (D, KVH * HD), (3.0 / D ** 0.5), 0.16699219, ((1, 4),)),
        "queries": draw_queries(jax.random.fold_in(key_of[9], 71), 0),
        "resp_keys": draw_resp_keys(jax.random.fold_in(key_of[9], 71), 0),
        "resp_values": gaussian(key_of[5], (RESPS, RLEN, KVH * HD), 3.0, 15.0, ((0, 64), (2, 4))),
        "lengths": draw_lengths(jax.random.fold_in(key_of[9], 71), 0),
        "assign": draw_assign(jax.random.fold_in(key_of[9], 71), 0),
        "grad_out": gaussian(key_of[8], (RESPS, RLEN, QH * HD), 1.0, 6.0, ((0, 64), (2, 4))),
    }


NEG_FILL = -1e+30

def one_response(query_in, prefix_k, prefix_v, own_keys, own_values, grad_in, length_now):
    total_keys = PLEN + RLEN
    key_all = jnp.concatenate([prefix_k, own_keys], 0).astype(jnp.float32).reshape(total_keys, KVH, HD)
    value_all = jnp.concatenate([prefix_v, own_values], 0).astype(jnp.float32).reshape(total_keys, KVH, HD)
    query_all = query_in.astype(jnp.float32).reshape(RLEN, KVH, GRP, HD)
    position = jnp.arange(RLEN, dtype=jnp.int32)
    resp_ok = (position[None, :] <= position[:, None]) & (position[None, :] < length_now)
    visible = jnp.concatenate([jnp.ones((RLEN, PLEN), dtype=jnp.bool_), resp_ok], 1)
    live = (position < length_now).astype(jnp.float32)[:, None, None, None]
    scale_factor = 1.0 / math.sqrt(HD)
    scores = jnp.einsum('tgjd,sgd->gjts', query_all, key_all) * scale_factor
    scores = jnp.where(visible[None, None], scores, NEG_FILL)
    row_top = lax.optimization_barrier(jnp.max(scores, -1, keepdims=True))
    exponent = jnp.exp(scores - row_top)
    weights = exponent / lax.optimization_barrier(jnp.sum(exponent, -1, keepdims=True))
    weights_low = lax.optimization_barrier(weights.astype(jnp.bfloat16)).astype(jnp.float32)
    output = jnp.einsum('gjts,sgd->tgjd', weights_low, value_all)
    attended = lax.optimization_barrier((output * live).astype(jnp.bfloat16))
    grad_live = grad_in.astype(jnp.float32).reshape(RLEN, KVH, GRP, HD) * live
    row_delta = lax.optimization_barrier(jnp.sum(grad_live * attended.astype(jnp.float32), -1))
    grad_weights = jnp.einsum('tgjd,sgd->gjts', grad_live, value_all)
    centred = grad_weights - jnp.transpose(row_delta, (1, 2, 0))[..., None]
    grad_scores = lax.optimization_barrier((weights * centred * scale_factor).astype(jnp.bfloat16)).astype(jnp.float32)
    query_grad = jnp.einsum('gjts,sgd->tgjd', grad_scores, key_all).astype(jnp.bfloat16).reshape(RLEN, QH * HD)
    key_grad = jnp.einsum('gjts,tgjd->sgd', grad_scores, query_all).reshape(total_keys, KVH * HD)
    value_grad = jnp.einsum('gjts,tgjd->sgd', weights_low, grad_live).reshape(total_keys, KVH * HD)
    return (attended.reshape(RLEN, QH * HD), query_grad, key_grad[:PLEN], value_grad[:PLEN], key_grad[PLEN:].astype(jnp.bfloat16), value_grad[PLEN:].astype(jnp.bfloat16))

def reference(prefix_hidden, w_key, w_value, queries, resp_keys, resp_values, lengths, assign, grad_out):
    prefix_k_all = jnp.dot(prefix_hidden, w_key, preferred_element_type=jnp.float32).astype(jnp.bfloat16)
    prefix_v_all = jnp.dot(prefix_hidden, w_value, preferred_element_type=jnp.float32).astype(jnp.bfloat16)
    kv_width = KVH * HD
    group_rows = PROM_GRP * PLEN

    def per_holder(running, holder):
        key_sum, value_sum = running
        group_row = (holder // N_RESP * group_rows).astype(jnp.int32)
        local_k = jnp.zeros((group_rows, kv_width), jnp.float32)
        local_v = jnp.zeros((group_rows, kv_width), jnp.float32)
        results = []
        for slot in range(RESP_DEV):
            resp_index = holder * RESP_DEV + slot
            start_row = (assign[resp_index] * PLEN).astype(jnp.int32)
            prefix_k = lax.dynamic_slice_in_dim(prefix_k_all, group_row + start_row, PLEN, 0)
            prefix_v = lax.dynamic_slice_in_dim(prefix_v_all, group_row + start_row, PLEN, 0)
            attended, query_grad, key_pref, value_pref, key_resp, value_resp = one_response(queries[resp_index], prefix_k, prefix_v, resp_keys[resp_index], resp_values[resp_index], grad_out[resp_index], lengths[resp_index])
            local_k = lax.dynamic_update_slice_in_dim(local_k, lax.dynamic_slice_in_dim(local_k, start_row, PLEN, 0) + key_pref, start_row, 0)
            local_v = lax.dynamic_update_slice_in_dim(local_v, lax.dynamic_slice_in_dim(local_v, start_row, PLEN, 0) + value_pref, start_row, 0)
            results.append((attended, query_grad, key_resp, value_resp))
        share_k = lax.optimization_barrier(local_k.astype(jnp.bfloat16)).astype(jnp.float32)
        share_v = lax.optimization_barrier(local_v.astype(jnp.bfloat16)).astype(jnp.float32)
        key_sum = lax.dynamic_update_slice_in_dim(key_sum, lax.dynamic_slice_in_dim(key_sum, group_row, group_rows, 0) + share_k, group_row, 0)
        value_sum = lax.dynamic_update_slice_in_dim(value_sum, lax.dynamic_slice_in_dim(value_sum, group_row, group_rows, 0) + share_v, group_row, 0)
        stacked_slots = tuple((jnp.stack([entry[index] for entry in results], 0) for index in range(4)))
        return ((key_sum, value_sum), stacked_slots)
    initial = (jnp.zeros((PROMPTS * PLEN, kv_width), jnp.float32), jnp.zeros((PROMPTS * PLEN, kv_width), jnp.float32))
    holders = RESPS // RESP_DEV
    (key_sum, value_sum), stacked = lax.scan(per_holder, initial, jnp.arange(holders, dtype=jnp.int32))
    attn_out, grad_query, grad_rkey, grad_rvalue = [item.reshape((RESPS,) + item.shape[2:]) for item in stacked]
    prefix_kgrad = key_sum.astype(jnp.bfloat16)
    prefix_vgrad = value_sum.astype(jnp.bfloat16)
    grad_wkey = jnp.dot(prefix_hidden.T, prefix_kgrad, preferred_element_type=jnp.float32)
    grad_wvalue = jnp.dot(prefix_hidden.T, prefix_vgrad, preferred_element_type=jnp.float32)
    return (attn_out, grad_query, grad_rkey, grad_rvalue, grad_wkey, grad_wvalue)
```

```python
import math

import jax
import jax.numpy as jnp
from jax import lax
from jax.experimental import pallas as pl
from jax.experimental.pallas import tpu as pltpu
from jax.sharding import PartitionSpec as P

HD = 128
PLEN = 1024
RLEN = 256
GRP = 5
NX = NY = 4
NZ = 2
NEG_FILL = -1e30
SCALE = 1.0 / math.sqrt(HD)
SCALE_LOG2E = SCALE * math.log2(math.e)
NT = (((1,), (1,)), ((), ()))
TN = (((0,), (0,)), ((), ()))
MESH = pl.DeviceIdType.MESH
F32 = jnp.float32
B16 = jnp.bfloat16
VMEM_LIMIT = 56 * 2**20


class Place:
    def __init__(self):
        self.p = lax.axis_index("prompt")
        self.r = lax.axis_index("resp")
        self.h = lax.axis_index("head")
        self.z = self.r // (NY * NX)
        self.y = lax.rem(self.r // NX, NY)
        self.x = lax.rem(self.r, NX)

    def at(self, z=None, y=None, x=None):
        z = self.z if z is None else z
        y = self.y if y is None else y
        x = self.x if x is None else x
        return (self.p, (z * NY + y) * NX + x, self.h)

    def head(self, step):
        return (self.p, self.r, lax.rem(self.h + step, 4))

    def core(self):
        return (1 - self.p, self.r, self.h)

    def plus(self, axis, step):
        return lax.rem((self.x if axis == "x" else self.y) + step, 4)

    def ring(self, axis, step):
        return self.at(**{axis: self.plus(axis, step)})


class Links:
    def __init__(self, send_sem, recv_sem):
        self.send_sem, self.recv_sem = send_sem, recv_sem
        self.count = 0
        self.open = []

    def send(self, src, dst, target):
        number = self.count
        self.count += 1
        copy = pltpu.make_async_remote_copy(
            src_ref=src, dst_ref=dst, send_sem=self.send_sem.at[number],
            recv_sem=self.recv_sem.at[number], device_id=target, device_id_type=MESH,
        )
        copy.start()
        self.open.append(copy)
        return number

    def landed(self, number, region, target):
        pltpu.make_async_remote_copy(
            src_ref=region, dst_ref=region, send_sem=self.send_sem.at[number],
            recv_sem=self.recv_sem.at[number], device_id=target, device_id_type=MESH,
        ).wait_recv()

    def drain(self):
        for copy in self.open:
            copy.wait_send()
        self.open = []


def greet(peers):
    barrier = pltpu.get_barrier_semaphore()
    for peer in peers:
        pl.semaphore_signal(barrier, inc=1, device_id=peer, device_id_type=MESH)
    pl.semaphore_wait(barrier, len(peers))


def ring_gather(links, place, axis, view):
    me, left, right, far = (place.plus(axis, s) for s in (0, 3, 1, 2))
    to_left, to_right = place.ring(axis, 3), place.ring(axis, 1)
    a = links.send(view(me, None), view(me, None), to_right)
    b = links.send(view(me, None), view(me, None), to_left)
    yield
    links.landed(a, view(left, None), to_left)
    c = links.send(view(left, 0), view(left, 0), to_right)
    links.landed(b, view(right, None), to_right)
    d = links.send(view(right, 1), view(right, 1), to_left)
    yield
    links.landed(c, view(far, 0), to_left)
    links.landed(d, view(far, 1), to_right)


def advance(steps):
    ended = object()
    return [g for g in steps if next(g, ended) is not ended]


def both(*steps):
    active = advance(steps)
    while active:
        yield
        active = advance(active)


def gather_rows(links, place, kview, vview):
    other = 1 - place.z
    partner = place.at(z=other)
    every = slice(None)
    pick = {0: pl.ds(0, 1), 1: pl.ds(1, 1), None: every}
    sent = [links.send(v(place.z, place.y, place.x), v(place.z, place.y, place.x), partner) for v in (kview, vview)]
    yield
    for number, v in zip(sent, (kview, vview)):
        links.landed(number, v(other, place.y, place.x), partner)
    yield from both(
        ring_gather(links, place, "y", lambda at, half: kview(pick[half], at, place.x)),
        ring_gather(links, place, "x", lambda at, half: vview(pick[half], place.y, at)),
    )
    yield from both(
        ring_gather(links, place, "x", lambda at, half: kview(pick[half], every, at)),
        ring_gather(links, place, "y", lambda at, half: vview(pick[half], at, every)),
    )


def run_all(steps):
    active, waiting = [], list(steps)
    while active or waiting:
        if waiting:
            active.append(waiting.pop(0))
        active = advance(active)


def project_kernel(hid, wk_hbm, wv_hbm, pk, pv, cols_out, hall, wk, wv, mine, turned, xbuf, wsem, send_sem, recv_sem, own_sem):
    place = Place()
    links = Links(send_sem, recv_sem)
    loads = [pltpu.make_async_copy(s, d, wsem.at[i]) for i, (s, d) in enumerate(((wk_hbm, wk), (wv_hbm, wv)))]
    for load in loads:
        load.start()
    partner = place.at(z=1 - place.z)
    to_left, to_right = place.head(3), place.head(1)
    greet([to_left, to_right, partner] + [place.ring(a, s) for a in "xy" for s in (1, 2, 3)])
    half = hid.shape[1] // 2
    lo, hi = pl.ds(0, half), pl.ds(half, half)
    own, low, high, far = (pl.ds(s, n) for s, n in ((0, 16), (16, 16), (32, 16), (48, 16)))
    a = links.send(hid.at[:, lo], hall.at[low, lo], to_right)
    b = links.send(hid.at[:, hi], hall.at[high, hi], to_left)
    c = links.send(hid.at[:, hi], hall.at[low, hi], to_right)
    d = links.send(hid.at[:, lo], hall.at[high, lo], to_left)
    hall[0:16] = hid[...]
    for load in loads:
        load.wait()

    def project(start, size):
        rows = hall[start:start + size]
        for w, out in ((wk, pk), (wv, pv)):
            out[place.z, place.y, place.x, start:start + size] = jnp.dot(
                rows, w[...], preferred_element_type=F32
            ).astype(B16)

    def gather(start, size):
        rows = pl.ds(start, size)
        return gather_rows(
            links, place,
            lambda z, y, x: pk.at[z, y, x, rows],
            lambda z, y, x: pv.at[z, y, x, rows],
        )

    project(0, 16)
    g0 = gather(0, 16)
    next(g0)
    links.landed(a, hall.at[low, lo], to_left)
    e = links.send(hall.at[low, lo], hall.at[far, lo], to_right)
    links.landed(b, hall.at[high, hi], to_right)
    f = links.send(hall.at[high, hi], hall.at[far, hi], to_left)
    next(g0)
    links.landed(c, hall.at[low, hi], to_left)
    links.landed(d, hall.at[high, lo], to_right)
    next(g0)
    project(16, 32)
    g1 = gather(16, 32)
    next(g1)
    next(g0)
    next(g1)
    links.landed(e, hall.at[far, lo], to_left)
    links.landed(f, hall.at[far, hi], to_right)
    project(48, 16)
    g2 = gather(48, 16)
    next(g2)

    width = half // NZ
    swap = []
    for p in range(2):
        src = hall.at[:, pl.ds(pl.multiple_of(p * half + (1 - place.z) * width, width), width)]
        swap.append((links.send(src, mine.at[p, place.z], partner), p))
        mine[p, place.z] = hall[:, pl.ds(pl.multiple_of(p * half + place.z * width, width), width)]
    run_all([g0, g1, g2])
    for number, p in swap:
        links.landed(number, mine.at[p, 1 - place.z], partner)
    for p in range(2):
        block = mine[p].reshape(mine.shape[1] * mine.shape[2], width)
        turned[p] = block.T.reshape(turned.shape[1:])
    sent = []
    for s in (1, 3, 2):
        to = place.plus("x", s)
        sent.append((s, links.send(turned.at[:, :, to], xbuf.at[place.x], place.ring("x", s))))
    keep = pltpu.make_async_copy(turned.at[:, :, place.x], xbuf.at[place.x], own_sem.at[0])
    keep.start()
    for s, number in sent:
        back = place.plus("x", 4 - s)
        links.landed(number, xbuf.at[back], place.ring("x", 4 - s))
    keep.wait()
    sent = []
    for s in (1, 3, 2):
        to = place.plus("y", s)
        sent.append((s, links.send(xbuf.at[:, :, to], cols_out.at[place.y], place.ring("y", s))))
    keep = pltpu.make_async_copy(xbuf.at[:, :, place.y], cols_out.at[place.y], own_sem.at[1])
    keep.start()
    for s, number in sent:
        back = place.plus("y", 4 - s)
        links.landed(number, cols_out.at[back], place.ring("y", 4 - s))
    keep.wait()
    links.drain()


def project(prefix_hidden, w_key, w_value):
    rows, depth = prefix_hidden.shape
    width = w_key.shape[1]
    block = depth // (2 * NZ * NY * NX)
    S = jax.ShapeDtypeStruct
    vm = pl.BlockSpec(memory_space=pltpu.VMEM)
    hbm = pl.BlockSpec(memory_space=pl.ANY)
    kv = S((NZ, NY, NX, 4 * rows, width), B16)
    copies = 6 + 3 * 18 + 2 + 6
    return pl.pallas_call(
        project_kernel,
        in_specs=[vm, hbm, hbm],
        out_specs=[vm, vm, vm],
        out_shape=[kv, kv, S((NY, NX, 2, block, 128), B16)],
        scratch_shapes=[
            pltpu.VMEM((4 * rows, depth), B16),
            pltpu.VMEM((depth, width), B16),
            pltpu.VMEM((depth, width), B16),
            pltpu.VMEM((2, NZ, 4 * rows, depth // 4), B16),
            pltpu.VMEM((2, NY, NX, block, 128), B16),
            pltpu.VMEM((NX, 2, NY, block, 128), B16),
            pltpu.SemaphoreType.DMA((2,)),
            pltpu.SemaphoreType.DMA((copies,)),
            pltpu.SemaphoreType.DMA((copies,)),
            pltpu.SemaphoreType.DMA((2,)),
        ],
        compiler_params=pltpu.CompilerParams(collective_id=0, has_side_effects=True, vmem_limit_bytes=VMEM_LIMIT),
        name="project",
    )(prefix_hidden, w_key, w_value)


def ring_reduce(links, place, axis, view, first, final, done):
    me, left, right, far = (place.plus(axis, s) for s in (0, 3, 1, 2))
    to_left, to_right = place.ring(axis, 3), place.ring(axis, 1)
    r0 = links.send(view(far, 0), first(0), to_right)
    l0 = links.send(view(far, 1), first(1), to_left)
    r1 = links.send(view(right, 1), final(0, 1), to_right)
    l1 = links.send(view(left, 0), final(1, 0), to_left)
    yield
    links.landed(r0, first(0), to_left)
    term = view(right, 0)
    term[...] = (term[...].astype(F32) + first(0)[...].astype(F32)).astype(B16)
    r2 = links.send(term, final(0, 0), to_right)
    links.landed(l0, first(1), to_right)
    term = view(left, 1)
    term[...] = (term[...].astype(F32) + first(1)[...].astype(F32)).astype(B16)
    l2 = links.send(term, final(1, 1), to_left)
    yield
    links.landed(r1, final(0, 1), to_left)
    links.landed(l1, final(1, 0), to_right)
    links.landed(r2, final(0, 0), to_left)
    links.landed(l2, final(1, 1), to_right)
    for half in range(2):
        total = view(me, half)[...].astype(F32)
        for side in range(2):
            total = total + final(side, half)[...].astype(F32)
        done(half, total)


def reduce_rows(links, place, kterm, vterm, buf1, buf2, mid, low, zbuf, put):
    every = slice(None)

    def store(ref):
        def done(half, total):
            ref[half] = total.astype(B16)
        return done

    yield from both(
        ring_reduce(links, place, "x", lambda at, half: kterm(half, every, at),
                    lambda d: buf1.at[0, d, 0], lambda d, half: buf1.at[0, d, 1 + half], store(mid.at[0])),
        ring_reduce(links, place, "y", lambda at, half: vterm(half, at, every),
                    lambda d: buf1.at[1, d, 0], lambda d, half: buf1.at[1, d, 1 + half], store(mid.at[1])),
    )
    yield from both(
        ring_reduce(links, place, "y", lambda at, half: mid.at[0, half, at],
                    lambda d: buf2.at[0, d, 0], lambda d, half: buf2.at[0, d, 1 + half], store(low.at[0])),
        ring_reduce(links, place, "x", lambda at, half: mid.at[1, half, at],
                    lambda d: buf2.at[1, d, 0], lambda d, half: buf2.at[1, d, 1 + half], store(low.at[1])),
    )
    partner = place.at(z=1 - place.z)
    sent = [links.send(low.at[w, 1 - place.z], zbuf.at[w], partner) for w in range(2)]
    yield
    for w, number in enumerate(sent):
        links.landed(number, zbuf.at[w], partner)
        put(w, (low[w, place.z].astype(F32) + zbuf[w].astype(F32)).astype(B16))


def grads_kernel(gk, gv, cols, wk_out, wv_out, buf1, buf2, mid, low, zbuf, gsum, theirs, landing, send_sem, recv_sem):
    place = Place()
    links = Links(send_sem, recv_sem)
    greet([place.core(), place.at(z=1 - place.z)] + [place.ring(a, s) for a in "xy" for s in (1, 3)])
    lhs = jnp.concatenate([cols[y, x].reshape(2 * cols.shape[3], 128) for y in range(NY) for x in range(NX)], axis=1)
    block = cols.shape[3]

    def chain(g):
        lanes = pl.ds(g * HD, HD)

        def put(which, total):
            gsum[g, which, place.y, place.x, place.z] = total

        yield from reduce_rows(
            links, place,
            lambda z, y, x: gk.at[z, y, x, :, lanes],
            lambda z, y, x: gv.at[z, y, x, :, lanes],
            buf1.at[g], buf2.at[g], mid.at[g], low.at[g], zbuf.at[g], put,
        )
        yield from gather_rows(
            links, place,
            lambda z, y, x: gsum.at[g, 0, y, x, z],
            lambda z, y, x: gsum.at[g, 1, y, x, z],
        )
        sent = []
        for which, out in ((0, wk_out), (1, wv_out)):
            rhs = gsum[g, which].reshape(NY * NX * NZ * gsum.shape[5], HD)
            product = jnp.dot(lhs, rhs, preferred_element_type=F32)
            theirs[g, which] = product.reshape(2, block, HD)
            sent.append(links.send(theirs.at[g, which, 1 - place.p], landing.at[g, which], place.core()))
        yield
        for which, out in ((0, wk_out), (1, wv_out)):
            links.landed(sent[which], landing.at[g, which], place.core())
            out[:, g * HD:(g + 1) * HD] = theirs[g, which, place.p] + landing[g, which]

    run_all([chain(0), chain(1)])
    links.drain()


def weight_grads(gk, gv, cols):
    width = gk.shape[-1]
    rows = gk.shape[3]
    kv = width // HD
    block = cols.shape[3]
    S = jax.ShapeDtypeStruct
    vm = pl.BlockSpec(memory_space=pltpu.VMEM)
    out = S((block, width), F32)
    copies = kv * (6 * 4 + 2 + 18 + 2)
    return pl.pallas_call(
        grads_kernel,
        in_specs=[vm, vm, vm],
        out_specs=[vm, vm],
        out_shape=[out, out],
        scratch_shapes=[
            pltpu.VMEM((kv, 2, 2, 3, 4, rows, HD), B16),
            pltpu.VMEM((kv, 2, 2, 3, rows, HD), B16),
            pltpu.VMEM((kv, 2, 2, 4, rows, HD), B16),
            pltpu.VMEM((kv, 2, 2, rows, HD), B16),
            pltpu.VMEM((kv, 2, rows, HD), B16),
            pltpu.VMEM((kv, 2, NY, NX, NZ, rows, HD), B16),
            pltpu.VMEM((kv, 2, 2, block, HD), F32),
            pltpu.VMEM((kv, 2, block, HD), F32),
            pltpu.SemaphoreType.DMA((copies,)),
            pltpu.SemaphoreType.DMA((copies,)),
        ],
        compiler_params=pltpu.CompilerParams(collective_id=1, has_side_effects=True, vmem_limit_bytes=VMEM_LIMIT),
        name="weight_grads",
    )(gk, gv, cols)


def attn_kernel(len_ref, asg_ref, q_ref, do_ref, rk_ref, rv_ref, pk_ref, pv_ref,
                o_ref, dq_ref, drk_ref, drv_ref, gk_ref, gv_ref,
                kall, vall, acck, accv):
    r = pl.program_id(1)
    length = len_ref[r]
    row0 = pl.multiple_of(asg_ref[r] * PLEN, PLEN)
    kall[:PLEN] = pk_ref[pl.ds(row0, PLEN), :]
    vall[:PLEN] = pv_ref[pl.ds(row0, PLEN), :]
    kall[PLEN:] = rk_ref[0]
    vall[PLEN:] = rv_ref[0]
    live = lax.broadcasted_iota(jnp.int32, (RLEN, 1), 0) < length
    causal = lax.broadcasted_iota(jnp.int32, (RLEN, RLEN), 1) <= lax.broadcasted_iota(jnp.int32, (RLEN, RLEN), 0)
    dkt = dvt = None
    for j in range(GRP):
        cols = slice(j * HD, (j + 1) * HD)
        q = q_ref[0, :, cols]
        k = kall[...]
        v = vall[...]
        s = lax.dot_general(q, k, NT, preferred_element_type=F32)
        s = jnp.concatenate([s[:, :PLEN], jnp.where(causal, s[:, PLEN:], NEG_FILL)], axis=1)
        top = jnp.max(s, axis=1, keepdims=True)
        e = jnp.exp2((s - top) * SCALE_LOG2E)
        inv = 1.0 / jnp.sum(e, axis=1, keepdims=True)
        inv = jnp.where(live, inv, 0.0)
        e_low = e.astype(B16)
        out = (jnp.dot(e_low, v, preferred_element_type=F32) * inv).astype(B16)
        o_ref[0, :, cols] = out
        g = (do_ref[0, :, cols].astype(F32) * inv).astype(B16)
        delta = jnp.sum(g.astype(F32) * out.astype(F32), axis=1, keepdims=True)
        dp = lax.dot_general(g, v, NT, preferred_element_type=F32)
        ds = (e * (dp - delta)).astype(B16)
        dq_ref[0, :, cols] = (jnp.dot(ds, k, preferred_element_type=F32) * SCALE).astype(B16)
        a = lax.dot_general(q, ds, TN, preferred_element_type=F32)
        b = lax.dot_general(g, e_low, TN, preferred_element_type=F32)
        dkt = a if j == 0 else dkt + a
        dvt = b if j == 0 else dvt + b
    dk = (dkt * SCALE).T
    dv = dvt.T
    drk_ref[0] = dk[PLEN:].astype(B16)
    drv_ref[0] = dv[PLEN:].astype(B16)

    @pl.when(r == 0)
    def _():
        acck[pl.ds(row0, PLEN), :] = dk[:PLEN]
        accv[pl.ds(row0, PLEN), :] = dv[:PLEN]
        other = pl.multiple_of(PLEN - row0, PLEN)
        acck[pl.ds(other, PLEN), :] = jnp.zeros((PLEN, HD), F32)
        accv[pl.ds(other, PLEN), :] = jnp.zeros((PLEN, HD), F32)

    @pl.when(r == 1)
    def _():
        acck[pl.ds(row0, PLEN), :] += dk[:PLEN]
        accv[pl.ds(row0, PLEN), :] += dv[:PLEN]
        gk_ref[...] = acck[...].astype(B16)
        gv_ref[...] = accv[...].astype(B16)


def attention(lengths, assign, queries, grad_out, resp_keys, resp_values, pk, pv):
    n = queries.shape[0]
    kv = resp_keys.shape[2] // HD
    rows = pk.shape[0]
    sm = pl.BlockSpec(memory_space=pltpu.SMEM)
    wide = pl.BlockSpec((1, RLEN, GRP * HD), lambda g, r: (r, 0, g))
    narrow = pl.BlockSpec((1, RLEN, HD), lambda g, r: (r, 0, g))
    prefix = pl.BlockSpec((rows, HD), lambda g, r: (0, g))
    S = jax.ShapeDtypeStruct
    return pl.pallas_call(
        attn_kernel,
        grid=(kv, n),
        in_specs=[sm, sm, wide, wide, narrow, narrow, prefix, prefix],
        out_specs=[wide, wide, narrow, narrow, prefix, prefix],
        out_shape=[S(queries.shape, B16), S(queries.shape, B16), S(resp_keys.shape, B16), S(resp_keys.shape, B16),
                   S((rows, kv * HD), B16), S((rows, kv * HD), B16)],
        scratch_shapes=[pltpu.VMEM((PLEN + RLEN, HD), B16), pltpu.VMEM((PLEN + RLEN, HD), B16),
                        pltpu.VMEM((rows, HD), F32), pltpu.VMEM((rows, HD), F32)],
        compiler_params=pltpu.CompilerParams(dimension_semantics=("arbitrary", "arbitrary"), vmem_limit_bytes=VMEM_LIMIT),
        name="attention",
    )(lengths, assign, queries, grad_out, resp_keys, resp_values, pk, pv)


def body(prefix_hidden, w_key, w_value, queries, resp_keys, resp_values, lengths, assign, grad_out):
    pk, pv, cols = project(prefix_hidden, w_key, w_value)
    flat = (NZ * PLEN, pk.shape[-1])
    o, dq, drk, drv, gk, gv = attention(
        lengths, assign, queries, grad_out, resp_keys, resp_values, pk.reshape(flat), pv.reshape(flat)
    )
    wk, wv = weight_grads(gk.reshape(pk.shape), gv.reshape(pv.shape), cols)
    return o, dq, drk, drv, wk, wv


def solution(mesh):
    return jax.shard_map(
        body,
        mesh=mesh,
        in_specs=(
            P(("prompt", "resp", "head"), None),
            P(None, "head"),
            P(None, "head"),
            P(("prompt", "resp"), None, "head"),
            P(("prompt", "resp"), None, "head"),
            P(("prompt", "resp"), None, "head"),
            P(("prompt", "resp")),
            P(("prompt", "resp")),
            P(("prompt", "resp"), None, "head"),
        ),
        out_specs=(
            P(("prompt", "resp"), None, "head"),
            P(("prompt", "resp"), None, "head"),
            P(("prompt", "resp"), None, "head"),
            P(("prompt", "resp"), None, "head"),
            P(("prompt", "resp"), "head"),
            P(("prompt", "resp"), "head"),
        ),
        check_vma=False,
    )
```

```python
import math

import jax
import jax.numpy as jnp
from jax import lax
from jax.experimental import pallas as pl
from jax.experimental.pallas import tpu as pltpu
from jax.sharding import PartitionSpec as P

HD = 128
PLEN = 1024
RLEN = 256
GRP = 5
NX = NY = 4
NZ = 2
NEG_FILL = -1e30
SCALE = 1.0 / math.sqrt(HD)
SCALE_LOG2E = SCALE * math.log2(math.e)
NT = (((1,), (1,)), ((), ()))
TN = (((0,), (0,)), ((), ()))
MESH = pl.DeviceIdType.MESH
F32 = jnp.float32
B16 = jnp.bfloat16
VMEM_LIMIT = 56 * 2**20


PLANE = ((0, 1), (0, 3), (1, 0), (1, 1), (1, 3), (0, 2), (1, 2))
RING = (1, 3, 2)
BLOCKS = 4


class Place:
    def __init__(self):
        self.p = lax.axis_index("prompt")
        self.r = lax.axis_index("resp")
        self.h = lax.axis_index("head")
        self.z = self.r // (NY * NX)
        self.y = lax.rem(self.r // NX, NY)
        self.x = lax.rem(self.r, NX)
        self.zs = [self.z, 1 - self.z]
        self.ys = [lax.rem(self.y + s, NY) for s in range(NY)]
        self.xs = [lax.rem(self.x + s, NX) for s in range(NX)]
        self.core = (1 - self.p, self.r, self.h)
        self.head = [(self.p, self.r, lax.rem(self.h + s, 4)) for s in range(4)]
        steps = [(0, s, 0) for s in range(NY)] + [(0, 0, s) for s in range(1, NX)]
        steps += [(1, s, 0) for s in range(NY)] + [(1, 0, s) for s in range(1, NX)]
        steps += [(0, s, t) for s in range(1, NY) for t in range(1, NX)]
        self.to = {
            (dz, dy, dx): (self.p, (self.zs[dz] * NY + self.ys[dy]) * NX + self.xs[dx], self.h)
            for dz, dy, dx in steps
        }

    def peers(self):
        return [self.core, self.head[1], self.head[3]] + [t for s, t in self.to.items() if s != (0, 0, 0)]


class Links:
    def __init__(self, send_sem, recv_sem):
        self.send_sem, self.recv_sem = send_sem, recv_sem
        self.count = 0

    def copy(self, number, src, dst, target):
        return pltpu.make_async_remote_copy(
            src_ref=src, dst_ref=dst, send_sem=self.send_sem.at[number],
            recv_sem=self.recv_sem.at[number], device_id=target, device_id_type=MESH,
        )

    def send(self, src, dst, target):
        number = self.count
        self.count += 1
        self.copy(number, src, dst, target).start()
        return number

    def landed(self, number, region, target):
        self.copy(number, region, region, target).wait()


def greet(peers):
    barrier = pltpu.get_barrier_semaphore()
    for peer in peers:
        pl.semaphore_signal(barrier, inc=1, device_id=peer, device_id_type=MESH)
    pl.semaphore_wait(barrier, len(peers))


def step_of(axis, dz, s):
    return (dz, s, 0) if axis == "y" else (dz, 0, s)


def along(place, axis, s):
    return (place.ys if axis == "y" else place.xs)[s]


def gather_rows(links, place, kview, vview):
    every = slice(None)
    sent = []
    for dz, s in PLANE:
        for axis, view in (("y", kview), ("x", vview)):
            own = view(place.z, place.y, place.x)
            sent.append((links.send(own, own, place.to[step_of(axis, dz, s)]), dz, s, axis, view))
    yield
    for number, dz, s, axis, view in sent:
        z, k = place.zs[dz], along(place, axis, (4 - s) % 4)
        region = view(z, k, place.x) if axis == "y" else view(z, place.y, k)
        links.landed(number, region, place.to[step_of(axis, dz, (4 - s) % 4)])
    sent = []
    for s in RING:
        for axis, view in (("x", kview), ("y", vview)):
            own = view(every, every, place.x) if axis == "x" else view(every, place.y, every)
            sent.append((links.send(own, own, place.to[step_of(axis, 0, s)]), s, axis, view))
    yield
    for number, s, axis, view in sent:
        k = along(place, axis, 4 - s)
        region = view(every, every, k) if axis == "x" else view(every, k, every)
        links.landed(number, region, place.to[step_of(axis, 0, 4 - s)])


def reduce_rows(links, place, kterm, vterm, buf1, buf2, mid, put):
    every = slice(None)
    sent = []
    for s in RING:
        for which, axis, term in ((0, "x", kterm), (1, "y", vterm)):
            k = along(place, axis, s)
            src = term(every, every, k) if axis == "x" else term(every, k, every)
            sent.append((links.send(src, buf1.at[which, s - 1], place.to[step_of(axis, 0, s)]), which, s, axis))
    yield
    for number, which, s, axis in sent:
        links.landed(number, buf1.at[which, s - 1], place.to[step_of(axis, 0, 4 - s)])
    for which, own in ((0, kterm(every, every, place.x)), (1, vterm(every, place.y, every))):
        total = own[...].astype(F32)
        for s in range(3):
            total = total + buf1[which, s].astype(F32)
        mid[which] = total.astype(B16)
    sent = []
    for i, (dz, s) in enumerate(PLANE):
        for which, axis in ((0, "y"), (1, "x")):
            src = mid.at[which, place.zs[dz], along(place, axis, s)]
            sent.append((links.send(src, buf2.at[which, i], place.to[step_of(axis, dz, s)]), which, i, axis, dz, s))
    yield
    for number, which, i, axis, dz, s in sent:
        links.landed(number, buf2.at[which, i], place.to[step_of(axis, dz, (4 - s) % 4)])
    for which, k in ((0, place.y), (1, place.x)):
        total = mid[which, place.z, k].astype(F32)
        for i in range(len(PLANE)):
            total = total + buf2[which, i].astype(F32)
        put(which, total.astype(B16))


def swap_columns(links, place, hall, mine, turned, cols):
    half = hall.shape[1] // 2
    width = half // NZ
    partner = place.to[(1, 0, 0)]
    sent = []
    for p in range(2):
        theirs = pl.ds(pl.multiple_of(p * half + place.zs[1] * width, width), width)
        sent.append((links.send(hall.at[:, theirs], mine.at[p, place.z], partner), p))
        ours = pl.ds(pl.multiple_of(p * half + place.z * width, width), width)
        mine[p, place.z] = hall[:, ours]
    yield
    for number, p in sent:
        links.landed(number, mine.at[p, place.zs[1]], partner)
    for p in range(2):
        block = mine[p].reshape(mine.shape[1] * mine.shape[2], width)
        turned[p] = block.T.reshape(turned.shape[1:])
    sent = []
    for dy in range(NY):
        for dx in range(NX):
            if dy or dx:
                number = links.send(
                    turned.at[:, place.ys[dy], place.xs[dx]], cols.at[place.y, place.x], place.to[(0, dy, dx)]
                )
                sent.append((number, dy, dx))
    for p in range(2):
        cols[place.y, place.x, p] = turned[p, place.y, place.x]
    yield
    for number, dy, dx in sent:
        dy, dx = (4 - dy) % 4, (4 - dx) % 4
        links.landed(number, cols.at[place.ys[dy], place.xs[dx]], place.to[(0, dy, dx)])


def layer_kernel(lengths, assign, hid, wk_hbm, wv_hbm, q_hbm, do_hbm, rk_hbm, rv_hbm,
                 o_hbm, dq_hbm, drk_hbm, drv_hbm, wk_out, wv_out,
                 hall, wk, wv, kbuf, vbuf, mine, turned, cols, lhs,
                 qb, gb, kall, vall, ob, dqb, drk, drv, dsb, erb, acck, accv, gk, gv,
                 buf1, buf2, mid, gsum, theirs, landing,
                 w_sem, in_sem, out_sem, send_sem, recv_sem):
    place = Place()
    links = Links(send_sem, recv_sem)
    wide = GRP * HD

    def part(ref, b, width):
        return ref.at[b % 2, :, pl.ds((b // 2) * width, width)]

    w_loads = [pltpu.make_async_copy(s, d, w_sem.at[i]) for i, (s, d) in enumerate(((wk_hbm, wk), (wv_hbm, wv)))]
    loads = []
    for b in range(BLOCKS):
        pairs = ((part(q_hbm, b, wide), qb.at[b]), (part(do_hbm, b, wide), gb.at[b]),
                 (part(rk_hbm, b, HD), kall.at[b, pl.ds(PLEN, RLEN)]), (part(rv_hbm, b, HD), vall.at[b, pl.ds(PLEN, RLEN)]))
        loads += [pltpu.make_async_copy(s, d, in_sem.at[4 * b + i]) for i, (s, d) in enumerate(pairs)]
    for load in w_loads + loads:
        load.start()
    greet(place.peers())

    to_left, to_right = place.head[3], place.head[1]
    half = hid.shape[1] // 2
    lo, hi = pl.ds(0, half), pl.ds(half, half)
    low, high, far = (pl.ds(s, 16) for s in (16, 32, 48))
    a = links.send(hid.at[:, lo], hall.at[low, lo], to_right)
    b = links.send(hid.at[:, hi], hall.at[high, hi], to_left)
    c = links.send(hid.at[:, hi], hall.at[low, hi], to_right)
    d = links.send(hid.at[:, lo], hall.at[high, lo], to_left)
    hall[0:16] = hid[...]
    for load in w_loads:
        load.wait()

    def project(start, size):
        rows = hall[start:start + size]
        for w, out in ((wk, kbuf), (wv, vbuf)):
            block = jnp.dot(rows, w[...], preferred_element_type=F32).astype(B16)
            for g in range(2):
                out[g, place.z, place.y, place.x, start:start + size] = block[:, g * HD:(g + 1) * HD]

    def gather(start, size, g):
        rows = pl.ds(start, size)
        return gather_rows(
            links, place,
            lambda z, y, x: kbuf.at[g, z, y, x, rows],
            lambda z, y, x: vbuf.at[g, z, y, x, rows],
        )

    every = slice(None)
    project(0, 16)
    first = gather(0, 16, every)
    next(first)
    links.landed(a, hall.at[low, lo], to_left)
    e = links.send(hall.at[low, lo], hall.at[far, lo], to_right)
    links.landed(b, hall.at[high, hi], to_right)
    f = links.send(hall.at[high, hi], hall.at[far, hi], to_left)
    next(first)
    links.landed(c, hall.at[low, hi], to_left)
    links.landed(d, hall.at[high, lo], to_right)
    project(16, 32)
    second = gather(16, 32, every)
    next(second)
    links.landed(e, hall.at[far, lo], to_left)
    links.landed(f, hall.at[far, hi], to_right)
    project(48, 16)
    third, fourth = gather(48, 16, 0), gather(48, 16, 1)
    next(third)
    next(second)
    next(fourth)
    swap = swap_columns(links, place, hall, mine, turned, cols)
    next(swap)
    for load in loads:
        load.wait()
    next(first, None)
    next(third)
    next(second, None)
    next(third, None)

    def terms(ref, g):
        return lambda z, y, x: ref.at[g, z, y, x]

    def put(g):
        def store(which, total):
            gsum[g, place.y, place.x, place.z, :, which * HD:(which + 1) * HD] = total
        return store

    def reduce(g):
        return reduce_rows(links, place, terms(gk, g), terms(gv, g), buf1.at[g], buf2.at[g], mid.at[g], put(g))

    def regather(g):
        return gather_rows(
            links, place,
            lambda z, y, x: gsum.at[g, y, x, z, :, pl.ds(0, HD)],
            lambda z, y, x: gsum.at[g, y, x, z, :, pl.ds(HD, HD)],
        )

    reduces = [reduce(0), reduce(1)]
    causal = lax.broadcasted_iota(jnp.int32, (RLEN, RLEN), 1) <= lax.broadcasted_iota(jnp.int32, (RLEN, RLEN), 0)

    def block(b, _):
        g, r = b // 2, lax.rem(b, 2)

        @pl.when(b == 1)
        def _():
            next(fourth)
            next(swap)

        @pl.when(b == 2)
        def _():
            next(reduces[0])
            next(fourth, None)

        is_first = assign[r] == 0
        live = lax.broadcasted_iota(jnp.int32, (RLEN, 1), 0) < lengths[r]
        for src, dst in ((kbuf, kall), (vbuf, vall)):
            dst[b, :PLEN] = jnp.where(is_first, src[g, 0].reshape(PLEN, HD), src[g, 1].reshape(PLEN, HD))
        dkt = dvt = None
        for j in range(GRP):
            lanes = slice(j * HD, (j + 1) * HD)
            q = qb[b, :, lanes]
            k = kall[b]
            v = vall[b]
            s = lax.dot_general(q, k, NT, preferred_element_type=F32)
            s = jnp.concatenate([s[:, :PLEN], jnp.where(causal, s[:, PLEN:], NEG_FILL)], axis=1)
            top = jnp.max(s, axis=1, keepdims=True)
            e = jnp.exp2((s - top) * SCALE_LOG2E)
            inv = 1.0 / jnp.sum(e, axis=1, keepdims=True)
            inv = jnp.where(live, inv, 0.0)
            e_low = e.astype(B16)
            out = (jnp.dot(e_low, v, preferred_element_type=F32) * inv).astype(B16)
            ob[b, :, lanes] = out
            grad = (gb[b, :, lanes].astype(F32) * inv).astype(B16)
            gb[b, :, lanes] = grad
            delta = jnp.sum(grad.astype(F32) * out.astype(F32), axis=1, keepdims=True)
            dp = lax.dot_general(grad, v, NT, preferred_element_type=F32)
            ds = (e * (dp - delta)).astype(B16)
            dsb[b, j] = ds
            erb[b, j] = e_low[:, PLEN:]
            kt = lax.dot_general(q, ds[:, :PLEN], TN, preferred_element_type=F32)
            vt = lax.dot_general(grad, e_low[:, :PLEN], TN, preferred_element_type=F32)
            dkt = kt if j == 0 else dkt + kt
            dvt = vt if j == 0 else dvt + vt
            if j == 2:
                @pl.when(b == 3)
                def _():
                    next(reduces[0])
        dk = (dkt * SCALE).T
        dv = dvt.T

        @pl.when(r == 0)
        def _():
            for i in range(2):
                mine_too = is_first if i == 0 else jnp.logical_not(is_first)
                acck[i] = jnp.where(mine_too, dk, 0.0)
                accv[i] = jnp.where(mine_too, dv, 0.0)

        @pl.when(r == 1)
        def _():
            for i in range(2):
                mine_too = is_first if i == 0 else jnp.logical_not(is_first)
                shape = gk.shape[2:]
                gk[g, i] = (acck[i] + jnp.where(mine_too, dk, 0.0)).astype(B16).reshape(shape)
                gv[g, i] = (accv[i] + jnp.where(mine_too, dv, 0.0)).astype(B16).reshape(shape)

        return 0

    lax.fori_loop(0, BLOCKS, block, 0)

    stores = []

    def store(number, src, dst):
        copy = pltpu.make_async_copy(src, dst, out_sem.at[number])
        copy.start()
        stores.append(copy)

    def late(b):
        dkt = dvt = None
        for j in range(GRP):
            lanes = slice(j * HD, (j + 1) * HD)
            dqb[b, :, lanes] = (jnp.dot(dsb[b, j], kall[b], preferred_element_type=F32) * SCALE).astype(B16)
            kt = lax.dot_general(qb[b, :, lanes], dsb[b, j, :, PLEN:], TN, preferred_element_type=F32)
            vt = lax.dot_general(gb[b, :, lanes], erb[b, j], TN, preferred_element_type=F32)
            dkt = kt if j == 0 else dkt + kt
            dvt = vt if j == 0 else dvt + vt
        drk[b] = (dkt * SCALE).T.astype(B16)
        drv[b] = dvt.T.astype(B16)
        store(4 * b, ob.at[b], part(o_hbm, b, wide))
        store(4 * b + 1, dqb.at[b], part(dq_hbm, b, wide))
        store(4 * b + 2, drk.at[b], part(drk_hbm, b, HD))
        store(4 * b + 3, drv.at[b], part(drv_hbm, b, HD))

    count = cols.shape[3]

    def product(g):
        rhs = gsum[g].reshape(NY * NX * NZ * gsum.shape[4], 2 * HD)
        theirs[g] = jnp.dot(lhs[...], rhs, preferred_element_type=F32).reshape(2, count, 2 * HD)
        return links.send(theirs.at[g, 1 - place.p], landing.at[g], place.core)

    def finish(g, number):
        links.landed(number, landing.at[g], place.core)
        total = theirs[g, place.p] + landing[g]
        wk_out[:, g * HD:(g + 1) * HD] = total[:, :HD]
        wv_out[:, g * HD:(g + 1) * HD] = total[:, HD:]

    next(reduces[1])
    late(0)
    next(reduces[0], None)
    regathers = [regather(0), regather(1)]
    next(regathers[0])
    late(1)
    next(swap, None)
    for y in range(NY):
        for x in range(NX):
            at = (y * NX + x) * HD
            lhs[:, at:at + HD] = cols[y, x].reshape(2 * count, HD)
    next(reduces[1])
    next(regathers[0])
    late(2)
    next(reduces[1], None)
    next(regathers[1])
    late(3)
    next(regathers[1])
    next(regathers[0], None)
    first_product = product(0)
    next(regathers[1], None)
    second_product = product(1)
    finish(0, first_product)
    finish(1, second_product)
    for copy in stores:
        copy.wait()


def layer(prefix_hidden, w_key, w_value, queries, resp_keys, resp_values, lengths, assign, grad_out):
    rows, depth = prefix_hidden.shape
    width = w_key.shape[1]
    count = depth // (2 * NZ * NY * NX)
    tall = 4 * rows
    S = jax.ShapeDtypeStruct
    vm = pl.BlockSpec(memory_space=pltpu.VMEM)
    sm = pl.BlockSpec(memory_space=pltpu.SMEM)
    hbm = pl.BlockSpec(memory_space=pl.ANY)
    V = pltpu.VMEM
    keys = PLEN + RLEN
    wide = GRP * HD
    copies = 192
    grads = S((count, width), F32)
    return pl.pallas_call(
        layer_kernel,
        in_specs=[sm, sm, vm] + [hbm] * 6,
        out_specs=[hbm] * 4 + [vm] * 2,
        out_shape=[S(queries.shape, B16), S(queries.shape, B16), S(resp_keys.shape, B16), S(resp_keys.shape, B16), grads, grads],
        scratch_shapes=[
            V((tall, depth), B16), V((depth, width), B16), V((depth, width), B16),
            V((2, NZ, NY, NX, tall, HD), B16), V((2, NZ, NY, NX, tall, HD), B16),
            V((2, NZ, tall, depth // 4), B16), V((2, NY, NX, count, HD), B16),
            V((NY, NX, 2, count, HD), B16), V((2 * count, NY * NX * HD), B16),
            V((BLOCKS, RLEN, wide), B16), V((BLOCKS, RLEN, wide), B16),
            V((BLOCKS, keys, HD), B16), V((BLOCKS, keys, HD), B16),
            V((BLOCKS, RLEN, wide), B16), V((BLOCKS, RLEN, wide), B16),
            V((BLOCKS, RLEN, HD), B16), V((BLOCKS, RLEN, HD), B16),
            V((BLOCKS, GRP, RLEN, keys), B16), V((BLOCKS, GRP, RLEN, RLEN), B16),
            V((2, PLEN, HD), F32), V((2, PLEN, HD), F32),
            V((2, NZ, NY, NX, tall, HD), B16), V((2, NZ, NY, NX, tall, HD), B16),
            V((2, 2, 3, NZ, 4, tall, HD), B16), V((2, 2, 7, tall, HD), B16), V((2, 2, NZ, 4, tall, HD), B16),
            V((2, NY, NX, NZ, tall, 2 * HD), B16),
            V((2, 2, count, 2 * HD), F32), V((2, count, 2 * HD), F32),
            pltpu.SemaphoreType.DMA((2,)), pltpu.SemaphoreType.DMA((4 * BLOCKS,)), pltpu.SemaphoreType.DMA((4 * BLOCKS,)),
            pltpu.SemaphoreType.DMA((copies,)), pltpu.SemaphoreType.DMA((copies,)),
        ],
        compiler_params=pltpu.CompilerParams(collective_id=0, has_side_effects=True, vmem_limit_bytes=VMEM_LIMIT),
        name="layer",
    )(lengths, assign, prefix_hidden, w_key, w_value, queries, grad_out, resp_keys, resp_values)


def hand_over_kernel(*refs):
    count = (len(refs) - 2) // 3
    sources, targets, held = refs[:count], refs[count:2 * count], refs[2 * count:3 * count]
    in_sem, out_sem = refs[3 * count:]
    reads, writes = [], []
    for i in range(count):
        for part in range(2):
            rows = pl.ds(part * (sources[i].shape[0] // 2), sources[i].shape[0] // 2)
            number = 2 * i + part
            reads.append(pltpu.make_async_copy(sources[i].at[rows], held[i].at[rows], in_sem.at[number]))
            writes.append(pltpu.make_async_copy(held[i].at[rows], targets[i].at[rows], out_sem.at[number]))
    for copy in reads:
        copy.start()
    for read, write in zip(reads, writes):
        read.wait()
        write.start()
    for copy in writes:
        copy.wait()


def hand_over(*arrays):
    hbm = pl.BlockSpec(memory_space=pl.ANY)
    return pl.pallas_call(
        hand_over_kernel,
        in_specs=[hbm] * len(arrays),
        out_specs=[hbm] * len(arrays),
        out_shape=[jax.ShapeDtypeStruct(a.shape, a.dtype) for a in arrays],
        scratch_shapes=[pltpu.VMEM(a.shape, a.dtype) for a in arrays]
        + [pltpu.SemaphoreType.DMA((2 * len(arrays),)), pltpu.SemaphoreType.DMA((2 * len(arrays),))],
        name="hand_over",
    )(*arrays)


def body(*arrays):
    return tuple(hand_over(*layer(*arrays)))


def solution(mesh):
    return jax.shard_map(
        body,
        mesh=mesh,
        in_specs=(
            P(("prompt", "resp", "head"), None),
            P(None, "head"),
            P(None, "head"),
            P(("prompt", "resp"), None, "head"),
            P(("prompt", "resp"), None, "head"),
            P(("prompt", "resp"), None, "head"),
            P(("prompt", "resp")),
            P(("prompt", "resp")),
            P(("prompt", "resp"), None, "head"),
        ),
        out_specs=(
            P(("prompt", "resp"), None, "head"),
            P(("prompt", "resp"), None, "head"),
            P(("prompt", "resp"), None, "head"),
            P(("prompt", "resp"), None, "head"),
            P(("prompt", "resp"), "head"),
            P(("prompt", "resp"), "head"),
        ),
        check_vma=False,
    )
```

```python
import math

import jax
import jax.numpy as jnp
from jax import lax
from jax.experimental import pallas as pl
from jax.experimental.pallas import tpu as pltpu
from jax.sharding import PartitionSpec as P

HD = 128
PLEN = 1024
RLEN = 256
GRP = 5
NX = NY = 4
NZ = 2
NEG_FILL = -1e30
SCALE = 1.0 / math.sqrt(HD)
SCALE_LOG2E = SCALE * math.log2(math.e)
NT = (((1,), (1,)), ((), ()))
TN = (((0,), (0,)), ((), ()))
MESH = pl.DeviceIdType.MESH
F32 = jnp.float32
B16 = jnp.bfloat16
VMEM_LIMIT = 56 * 2**20


PLANE = ((0, 1), (0, 3), (1, 0), (1, 1), (1, 3), (0, 2), (1, 2))
RING = (1, 3, 2)
BLOCKS = 4


class Place:
    def __init__(self):
        self.p = lax.axis_index("prompt")
        self.r = lax.axis_index("resp")
        self.h = lax.axis_index("head")
        self.z = self.r // (NY * NX)
        self.y = lax.rem(self.r // NX, NY)
        self.x = lax.rem(self.r, NX)
        self.zs = [self.z, 1 - self.z]
        self.ys = [lax.rem(self.y + s, NY) for s in range(NY)]
        self.xs = [lax.rem(self.x + s, NX) for s in range(NX)]
        self.cores = [self.p, 1 - self.p]
        self.core = (1 - self.p, self.r, self.h)
        self.head = [(self.p, self.r, lax.rem(self.h + s, 4)) for s in range(4)]
        steps = [(0, s, 0) for s in range(NY)] + [(0, 0, s) for s in range(1, NX)]
        steps += [(1, s, 0) for s in range(NY)] + [(1, 0, s) for s in range(1, NX)]
        self.to = {
            (dz, dy, dx): (self.p, (self.zs[dz] * NY + self.ys[dy]) * NX + self.xs[dx], self.h)
            for dz, dy, dx in steps
        }

    def peers(self):
        near = [t for s, t in self.to.items() if s != (0, 0, 0)]
        across = [(self.cores[1], *self.to[step_of(axis, 0, s)][1:]) for axis in "xy" for s in RING]
        return [self.core, self.head[1], self.head[3]] + near + across


class Links:
    def __init__(self, send_sem, recv_sem):
        self.send_sem, self.recv_sem = send_sem, recv_sem
        self.count = 0

    def copy(self, number, src, dst, target):
        return pltpu.make_async_remote_copy(
            src_ref=src, dst_ref=dst, send_sem=self.send_sem.at[number],
            recv_sem=self.recv_sem.at[number], device_id=target, device_id_type=MESH,
        )

    def send(self, src, dst, target):
        number = self.count
        self.count += 1
        self.copy(number, src, dst, target).start()
        return number

    def landed(self, number, region, target):
        self.copy(number, region, region, target).wait()


def greet(peers):
    barrier = pltpu.get_barrier_semaphore()
    for peer in peers:
        pl.semaphore_signal(barrier, inc=1, device_id=peer, device_id_type=MESH)
    pl.semaphore_wait(barrier, len(peers))


def step_of(axis, dz, s):
    return (dz, s, 0) if axis == "y" else (dz, 0, s)


def along(place, axis, s):
    return (place.ys if axis == "y" else place.xs)[s]


def gather_rows(links, place, kview, vview):
    every = slice(None)
    sent = []
    for dz, s in PLANE:
        for axis, view in (("y", kview), ("x", vview)):
            own = view(place.z, place.y, place.x)
            sent.append((links.send(own, own, place.to[step_of(axis, dz, s)]), dz, s, axis, view))
    yield
    for number, dz, s, axis, view in sent:
        z, k = place.zs[dz], along(place, axis, (4 - s) % 4)
        region = view(z, k, place.x) if axis == "y" else view(z, place.y, k)
        links.landed(number, region, place.to[step_of(axis, dz, (4 - s) % 4)])
    sent = []
    for s in RING:
        for axis, view in (("x", kview), ("y", vview)):
            own = view(every, every, place.x) if axis == "x" else view(every, place.y, every)
            sent.append((links.send(own, own, place.to[step_of(axis, 0, s)]), s, axis, view))
    yield
    for number, s, axis, view in sent:
        k = along(place, axis, 4 - s)
        region = view(every, every, k) if axis == "x" else view(every, k, every)
        links.landed(number, region, place.to[step_of(axis, 0, 4 - s)])


def gather_rows_late(links, place, kview, vview):
    every = slice(None)
    partner = place.to[(1, 0, 0)]
    sent = []
    for view in (kview, vview):
        own = view(place.z, place.y, place.x)
        sent.append((links.send(own, own, partner), view))
    yield
    for number, view in sent:
        links.landed(number, view(place.zs[1], place.y, place.x), partner)
    for stage in range(2):
        sent = []
        for s in RING:
            for axis, view in (("yx"[stage], kview), ("xy"[stage], vview)):
                def region(k, axis=axis, view=view):
                    if stage == 0:
                        return view(every, k, place.x) if axis == "y" else view(every, place.y, k)
                    return view(every, k, every) if axis == "y" else view(every, every, k)
                own = region(along(place, axis, 0))
                sent.append((links.send(own, own, place.to[step_of(axis, 0, s)]), s, axis, region))
        yield
        for number, s, axis, region in sent:
            links.landed(number, region(along(place, axis, 4 - s)), place.to[step_of(axis, 0, 4 - s)])


def gather_plane(links, place, kview, vview):
    sent = []
    for dz, s in PLANE:
        for axis, view in (("y", kview), ("x", vview)):
            own = view(place.z, along(place, axis, 0))
            sent.append((links.send(own, own, place.to[step_of(axis, dz, s)]), dz, s, axis, view))
    yield
    for number, dz, s, axis, view in sent:
        back = (4 - s) % 4
        links.landed(number, view(place.zs[dz], along(place, axis, back)), place.to[step_of(axis, dz, back)])


def reduce_products(links, place, theirs, landing, done):
    sent = []
    for s in (2, 1, 3, 0):
        for core in (1, 0):
            if core or s:
                for which, axis in ((0, "x"), (1, "y")):
                    slot = 4 * core + s - 1
                    target = place.to[step_of(axis, 0, s)]
                    target = (place.cores[core], *target[1:])
                    number = links.send(theirs.at[which, core, s], landing.at[which, slot], target)
                    sent.append((number, which, axis, s, core, slot))
    yield
    for number, which, axis, s, core, slot in sent:
        target = place.to[step_of(axis, 0, (4 - s) % 4)]
        links.landed(number, landing.at[which, slot], (place.cores[core], *target[1:]))
    for which in range(2):
        total = theirs[which, 0, 0].astype(F32)
        for slot in range(7):
            total = total + landing[which, slot].astype(F32)
        done(which, total)


def reduce_rows(links, place, kterm, vterm, buf1, buf2, mid, put):
    every = slice(None)
    sent = []
    for s in RING:
        for which, axis, term in ((0, "x", kterm), (1, "y", vterm)):
            k = along(place, axis, s)
            src = term(every, every, k) if axis == "x" else term(every, k, every)
            sent.append((links.send(src, buf1.at[which, s - 1], place.to[step_of(axis, 0, s)]), which, s, axis))
    yield
    for number, which, s, axis in sent:
        links.landed(number, buf1.at[which, s - 1], place.to[step_of(axis, 0, 4 - s)])
    for which, own in ((0, kterm(every, every, place.x)), (1, vterm(every, place.y, every))):
        total = own[...].astype(F32)
        for s in range(3):
            total = total + buf1[which, s].astype(F32)
        mid[which] = total.astype(B16)
    sent = []
    for i, (dz, s) in enumerate(PLANE):
        for which, axis in ((0, "y"), (1, "x")):
            src = mid.at[which, place.zs[dz], along(place, axis, s)]
            sent.append((links.send(src, buf2.at[which, i], place.to[step_of(axis, dz, s)]), which, i, axis, dz, s))
    yield
    for number, which, i, axis, dz, s in sent:
        links.landed(number, buf2.at[which, i], place.to[step_of(axis, dz, (4 - s) % 4)])
    for which, k in ((0, place.y), (1, place.x)):
        total = mid[which, place.z, k].astype(F32)
        for i in range(len(PLANE)):
            total = total + buf2[which, i].astype(F32)
        put(which, total.astype(B16))


def swap_columns(links, place, hall, mine, turned, cols):
    half = hall.shape[1] // 2
    width = half // NZ
    partner = place.to[(1, 0, 0)]
    sent = []
    for p in range(2):
        theirs = pl.ds(pl.multiple_of(p * half + place.zs[1] * width, width), width)
        sent.append((links.send(hall.at[:, theirs], mine.at[p, place.z], partner), p))
        ours = pl.ds(pl.multiple_of(p * half + place.z * width, width), width)
        mine[p, place.z] = hall[:, ours]
    yield
    for number, p in sent:
        links.landed(number, mine.at[p, place.zs[1]], partner)
    for p in range(2):
        block = mine[p].reshape(mine.shape[1] * mine.shape[2], width)
        turned[p] = block.T.reshape(turned.shape[1:])
    sent = []
    for s in RING:
        for which, axis in ((0, "y"), (1, "x")):
            src = turned.at[:, place.ys[s]] if axis == "y" else turned.at[:, :, place.xs[s]]
            number = links.send(src, cols.at[which, along(place, axis, 0)], place.to[step_of(axis, 0, s)])
            sent.append((number, which, axis, s))
    for p in range(2):
        cols[0, place.y, p] = turned[p, place.y]
        for k in range(4):
            cols[1, place.x, p, k] = turned[p, k, place.x]
    yield
    for number, which, axis, s in sent:
        links.landed(number, cols.at[which, along(place, axis, 4 - s)], place.to[step_of(axis, 0, 4 - s)])


def layer_kernel(lengths, assign, hid, wk_hbm, wv_hbm, q_hbm, do_hbm, rk_hbm, rv_hbm,
                 o_hbm, dq_hbm, drk_hbm, drv_hbm, wk_out, wv_out,
                 hall, wk, wv, kbuf, vbuf, mine, turned, cols, lhs,
                 qb, gb, kall, vall, ob, dqb, drk, drv, dsb, erb, acck, accv, gk, gv,
                 buf1, buf2, mid, gsum, spread, theirs, landing,
                 w_sem, in_sem, out_sem, send_sem, recv_sem):
    place = Place()
    links = Links(send_sem, recv_sem)
    wide = GRP * HD

    def part(ref, b, width):
        return ref.at[b % 2, :, pl.ds((b // 2) * width, width)]

    w_loads = [pltpu.make_async_copy(s, d, w_sem.at[i]) for i, (s, d) in enumerate(((wk_hbm, wk), (wv_hbm, wv)))]
    loads = []
    for b in range(BLOCKS):
        pairs = ((part(q_hbm, b, wide), qb.at[b]), (part(do_hbm, b, wide), gb.at[b]),
                 (part(rk_hbm, b, HD), kall.at[b, pl.ds(PLEN, RLEN)]), (part(rv_hbm, b, HD), vall.at[b, pl.ds(PLEN, RLEN)]))
        loads += [pltpu.make_async_copy(s, d, in_sem.at[4 * b + i]) for i, (s, d) in enumerate(pairs)]
    for load in w_loads + loads:
        load.start()
    greet(place.peers())

    to_left, to_right = place.head[3], place.head[1]
    half = hid.shape[1] // 2
    lo, hi = pl.ds(0, half), pl.ds(half, half)
    low, high, far = (pl.ds(s, 16) for s in (16, 32, 48))
    a = links.send(hid.at[:, lo], hall.at[low, lo], to_right)
    b = links.send(hid.at[:, hi], hall.at[high, hi], to_left)
    c = links.send(hid.at[:, hi], hall.at[low, hi], to_right)
    d = links.send(hid.at[:, lo], hall.at[high, lo], to_left)
    hall[0:16] = hid[...]
    for load in w_loads:
        load.wait()

    def project(start, size):
        rows = hall[start:start + size]
        for w, out in ((wk, kbuf), (wv, vbuf)):
            block = jnp.dot(rows, w[...], preferred_element_type=F32).astype(B16)
            for g in range(2):
                out[g, place.z, place.y, place.x, start:start + size] = block[:, g * HD:(g + 1) * HD]

    def gather(how, start, size, g):
        rows = pl.ds(start, size)
        return how(
            links, place,
            lambda z, y, x: kbuf.at[g, z, y, x, rows],
            lambda z, y, x: vbuf.at[g, z, y, x, rows],
        )

    every = slice(None)
    project(0, 16)
    first = gather(gather_rows_late, 0, 16, every)
    next(first)
    links.landed(a, hall.at[low, lo], to_left)
    e = links.send(hall.at[low, lo], hall.at[far, lo], to_right)
    links.landed(b, hall.at[high, hi], to_right)
    f = links.send(hall.at[high, hi], hall.at[far, hi], to_left)
    next(first)
    links.landed(c, hall.at[low, hi], to_left)
    links.landed(d, hall.at[high, lo], to_right)
    project(16, 32)
    second = gather(gather_rows_late, 16, 32, every)
    next(second)
    next(first)
    next(second)
    links.landed(e, hall.at[far, lo], to_left)
    links.landed(f, hall.at[far, hi], to_right)
    project(48, 16)
    third, fourth = gather(gather_rows, 48, 16, 0), gather(gather_rows, 48, 16, 1)
    next(third)
    next(fourth)
    swap = swap_columns(links, place, hall, mine, turned, cols)
    next(swap)
    next(second)
    next(third)
    for load in loads:
        load.wait()
    next(first, None)
    next(second, None)
    next(third, None)

    count = cols.shape[4]
    outs = (wk_out, wv_out)

    def chain(g):
        return run_chain(g, gsum.at[g], buf1.at[g], buf2.at[g], mid.at[g], theirs.at[g], landing.at[g])

    def run_chain(g, total, first_landing, second_landing, between, own, last_landing):
        def put(which, value):
            total[which, along(place, "yx"[which], 0), place.z] = value

        yield from reduce_rows(
            links, place,
            lambda z, y, x: gk.at[g, z, y, x],
            lambda z, y, x: gv.at[g, z, y, x],
            first_landing, second_landing, between, put,
        )
        yield from gather_plane(
            links, place,
            lambda z, y: total.at[0, y, z],
            lambda z, x: total.at[1, x, z],
        )
        for which, axis in ((0, "x"), (1, "y")):
            rhs = total[which].reshape(-1, HD)
            product = jnp.dot(lhs[which], rhs, preferred_element_type=F32).astype(B16)
            spread[g, which] = product.reshape(spread.shape[2:])
            for core in range(2):
                for s in range(4):
                    k = along(place, axis, s)
                    own[which, core, s] = spread[g, which, place.cores[core], k]

        def done(which, value):
            outs[which][:, g * HD:(g + 1) * HD] = value

        yield from reduce_products(links, place, own, last_landing, done)

    chains = [chain(0), chain(1)]
    causal = lax.broadcasted_iota(jnp.int32, (RLEN, RLEN), 1) <= lax.broadcasted_iota(jnp.int32, (RLEN, RLEN), 0)

    def block(b, _):
        g, r = b // 2, lax.rem(b, 2)

        @pl.when(b == 1)
        def _():
            next(fourth)
            next(swap)

        @pl.when(b == 2)
        def _():
            next(chains[0])
            next(fourth, None)

        is_first = assign[r] == 0
        live = lax.broadcasted_iota(jnp.int32, (RLEN, 1), 0) < lengths[r]
        for src, dst in ((kbuf, kall), (vbuf, vall)):
            dst[b, :PLEN] = jnp.where(is_first, src[g, 0].reshape(PLEN, HD), src[g, 1].reshape(PLEN, HD))
        dkt = dvt = None

        def scores(j):
            s = lax.dot_general(qb[b, :, j * HD:(j + 1) * HD], kall[b], NT, preferred_element_type=F32)
            return jnp.concatenate([s[:, :PLEN], jnp.where(causal, s[:, PLEN:], NEG_FILL)], axis=1)

        following = scores(0)
        for j in range(GRP):
            lanes = slice(j * HD, (j + 1) * HD)
            q = qb[b, :, lanes]
            v = vall[b]
            s = following
            if j + 1 < GRP:
                following = scores(j + 1)
            top = jnp.max(s, axis=1, keepdims=True)
            e = jnp.exp2((s - top) * SCALE_LOG2E)
            inv = 1.0 / jnp.sum(e, axis=1, keepdims=True)
            inv = jnp.where(live, inv, 0.0)
            e_low = e.astype(B16)
            out = (jnp.dot(e_low, v, preferred_element_type=F32) * inv).astype(B16)
            ob[b, :, lanes] = out
            grad = (gb[b, :, lanes].astype(F32) * inv).astype(B16)
            gb[b, :, lanes] = grad
            delta = jnp.sum(grad.astype(F32) * out.astype(F32), axis=1, keepdims=True)
            dp = lax.dot_general(grad, v, NT, preferred_element_type=F32)
            ds = (e * (dp - delta)).astype(B16)
            dsb[b, j] = ds
            erb[b, j] = e_low[:, PLEN:]
            kt = lax.dot_general(q, ds[:, :PLEN], TN, preferred_element_type=F32)
            vt = lax.dot_general(grad, e_low[:, :PLEN], TN, preferred_element_type=F32)
            dkt = kt if j == 0 else dkt + kt
            dvt = vt if j == 0 else dvt + vt
            if j == 2:
                @pl.when(b == 3)
                def _():
                    next(chains[0])
        dk = (dkt * SCALE).T
        dv = dvt.T

        @pl.when(r == 0)
        def _():
            for i in range(2):
                mine_too = is_first if i == 0 else jnp.logical_not(is_first)
                acck[i] = jnp.where(mine_too, dk, 0.0)
                accv[i] = jnp.where(mine_too, dv, 0.0)

        @pl.when(r == 1)
        def _():
            for i in range(2):
                mine_too = is_first if i == 0 else jnp.logical_not(is_first)
                shape = gk.shape[2:]
                gk[g, i] = (acck[i] + jnp.where(mine_too, dk, 0.0)).astype(B16).reshape(shape)
                gv[g, i] = (accv[i] + jnp.where(mine_too, dv, 0.0)).astype(B16).reshape(shape)

        return 0

    lax.fori_loop(0, BLOCKS, block, 0)

    stores = []

    def store(number, src, dst):
        copy = pltpu.make_async_copy(src, dst, out_sem.at[number])
        copy.start()
        stores.append(copy)

    def late(b):
        dkt = dvt = None
        for j in range(GRP):
            lanes = slice(j * HD, (j + 1) * HD)
            dqb[b, :, lanes] = (jnp.dot(dsb[b, j], kall[b], preferred_element_type=F32) * SCALE).astype(B16)
            kt = lax.dot_general(qb[b, :, lanes], dsb[b, j, :, PLEN:], TN, preferred_element_type=F32)
            vt = lax.dot_general(gb[b, :, lanes], erb[b, j], TN, preferred_element_type=F32)
            dkt = kt if j == 0 else dkt + kt
            dvt = vt if j == 0 else dvt + vt
        drk[b] = (dkt * SCALE).T.astype(B16)
        drv[b] = dvt.T.astype(B16)
        store(4 * b, ob.at[b], part(o_hbm, b, wide))
        store(4 * b + 1, dqb.at[b], part(dq_hbm, b, wide))
        store(4 * b + 2, drk.at[b], part(drk_hbm, b, HD))
        store(4 * b + 3, drv.at[b], part(drv_hbm, b, HD))

    next(chains[1])
    late(0)
    next(chains[0])
    next(swap, None)
    for which in range(2):
        for k in range(4):
            lhs[which, :, k * HD:(k + 1) * HD] = cols[which, k].reshape(lhs.shape[1], HD)
    late(1)
    next(chains[1])
    next(chains[0])
    late(2)
    next(chains[1])
    late(3)
    next(chains[1])
    next(chains[0], None)
    next(chains[1], None)
    for copy in stores:
        copy.wait()


def layer(prefix_hidden, w_key, w_value, queries, resp_keys, resp_values, lengths, assign, grad_out):
    rows, depth = prefix_hidden.shape
    width = w_key.shape[1]
    count = depth // (2 * NZ * NY * NX)
    tall = 4 * rows
    S = jax.ShapeDtypeStruct
    vm = pl.BlockSpec(memory_space=pltpu.VMEM)
    sm = pl.BlockSpec(memory_space=pltpu.SMEM)
    hbm = pl.BlockSpec(memory_space=pl.ANY)
    V = pltpu.VMEM
    keys = PLEN + RLEN
    wide = GRP * HD
    copies = 192
    grads = S((count, width), F32)
    return pl.pallas_call(
        layer_kernel,
        in_specs=[sm, sm, vm] + [hbm] * 6,
        out_specs=[hbm] * 4 + [vm] * 2,
        out_shape=[S(queries.shape, B16), S(queries.shape, B16), S(resp_keys.shape, B16), S(resp_keys.shape, B16), grads, grads],
        scratch_shapes=[
            V((tall, depth), B16), V((depth, width), B16), V((depth, width), B16),
            V((2, NZ, NY, NX, tall, HD), B16), V((2, NZ, NY, NX, tall, HD), B16),
            V((2, NZ, tall, depth // 4), B16), V((2, NY, NX, count, HD), B16),
            V((2, 4, 2, 4, count, HD), B16), V((2, 8 * count, 4 * HD), B16),
            V((BLOCKS, RLEN, wide), B16), V((BLOCKS, RLEN, wide), B16),
            V((BLOCKS, keys, HD), B16), V((BLOCKS, keys, HD), B16),
            V((BLOCKS, RLEN, wide), B16), V((BLOCKS, RLEN, wide), B16),
            V((BLOCKS, RLEN, HD), B16), V((BLOCKS, RLEN, HD), B16),
            V((BLOCKS, GRP, RLEN, keys), B16), V((BLOCKS, GRP, RLEN, RLEN), B16),
            V((2, PLEN, HD), F32), V((2, PLEN, HD), F32),
            V((2, NZ, NY, NX, tall, HD), B16), V((2, NZ, NY, NX, tall, HD), B16),
            V((2, 2, 3, NZ, 4, tall, HD), B16), V((2, 2, 7, tall, HD), B16), V((2, 2, NZ, 4, tall, HD), B16),
            V((2, 2, 4, NZ, tall, HD), B16), V((2, 2, 2, 4, count, HD), B16),
            V((2, 2, 2, 4, count, HD), B16), V((2, 2, 7, count, HD), B16),
            pltpu.SemaphoreType.DMA((2,)), pltpu.SemaphoreType.DMA((4 * BLOCKS,)), pltpu.SemaphoreType.DMA((4 * BLOCKS,)),
            pltpu.SemaphoreType.DMA((copies,)), pltpu.SemaphoreType.DMA((copies,)),
        ],
        compiler_params=pltpu.CompilerParams(collective_id=0, has_side_effects=True, vmem_limit_bytes=VMEM_LIMIT),
        name="layer",
    )(lengths, assign, prefix_hidden, w_key, w_value, queries, grad_out, resp_keys, resp_values)


def hand_over_kernel(*refs):
    count = (len(refs) - 2) // 3
    sources, targets, held = refs[:count], refs[count:2 * count], refs[2 * count:3 * count]
    in_sem, out_sem = refs[3 * count:]
    reads, writes = [], []
    for i in range(count):
        for part in range(2):
            rows = pl.ds(part * (sources[i].shape[0] // 2), sources[i].shape[0] // 2)
            number = 2 * i + part
            reads.append(pltpu.make_async_copy(sources[i].at[rows], held[i].at[rows], in_sem.at[number]))
            writes.append(pltpu.make_async_copy(held[i].at[rows], targets[i].at[rows], out_sem.at[number]))
    for copy in reads:
        copy.start()
    for read, write in zip(reads, writes):
        read.wait()
        write.start()
    for copy in writes:
        copy.wait()


def hand_over(*arrays):
    hbm = pl.BlockSpec(memory_space=pl.ANY)
    return pl.pallas_call(
        hand_over_kernel,
        in_specs=[hbm] * len(arrays),
        out_specs=[hbm] * len(arrays),
        out_shape=[jax.ShapeDtypeStruct(a.shape, a.dtype) for a in arrays],
        scratch_shapes=[pltpu.VMEM(a.shape, a.dtype) for a in arrays]
        + [pltpu.SemaphoreType.DMA((2 * len(arrays),)), pltpu.SemaphoreType.DMA((2 * len(arrays),))],
        name="hand_over",
    )(*arrays)


def body(*arrays):
    return tuple(hand_over(*layer(*arrays)))


def solution(mesh):
    return jax.shard_map(
        body,
        mesh=mesh,
        in_specs=(
            P(("prompt", "resp", "head"), None),
            P(None, "head"),
            P(None, "head"),
            P(("prompt", "resp"), None, "head"),
            P(("prompt", "resp"), None, "head"),
            P(("prompt", "resp"), None, "head"),
            P(("prompt", "resp")),
            P(("prompt", "resp")),
            P(("prompt", "resp"), None, "head"),
        ),
        out_specs=(
            P(("prompt", "resp"), None, "head"),
            P(("prompt", "resp"), None, "head"),
            P(("prompt", "resp"), None, "head"),
            P(("prompt", "resp"), None, "head"),
            P(("prompt", "resp"), "head"),
            P(("prompt", "resp"), "head"),
        ),
        check_vma=False,
    )
```

```python
import math

import jax
import jax.numpy as jnp
from jax import lax
from jax.experimental import pallas as pl
from jax.experimental.pallas import tpu as pltpu
from jax.sharding import PartitionSpec as P

HD = 128
PLEN = 1024
RLEN = 256
GRP = 5
NX = NY = 4
NZ = 2
NEG_FILL = -1e30
SCALE = 1.0 / math.sqrt(HD)
SCALE_LOG2E = SCALE * math.log2(math.e)
NT = (((1,), (1,)), ((), ()))
TN = (((0,), (0,)), ((), ()))
MESH = pl.DeviceIdType.MESH
F32 = jnp.float32
B16 = jnp.bfloat16
VMEM_LIMIT = 56 * 2**20


PLANE = ((0, 1), (0, 3), (1, 0), (1, 1), (1, 3), (0, 2), (1, 2))
RING = (1, 3, 2)
BLOCKS = 4


class Place:
    def __init__(self):
        self.p = lax.axis_index("prompt")
        self.r = lax.axis_index("resp")
        self.h = lax.axis_index("head")
        self.z = self.r // (NY * NX)
        self.y = lax.rem(self.r // NX, NY)
        self.x = lax.rem(self.r, NX)
        self.zs = [self.z, 1 - self.z]
        self.ys = [lax.rem(self.y + s, NY) for s in range(NY)]
        self.xs = [lax.rem(self.x + s, NX) for s in range(NX)]
        self.cores = [self.p, 1 - self.p]
        self.core = (1 - self.p, self.r, self.h)
        self.head = [(self.p, self.r, lax.rem(self.h + s, 4)) for s in range(4)]
        steps = [(0, s, 0) for s in range(NY)] + [(0, 0, s) for s in range(1, NX)]
        steps += [(1, s, 0) for s in range(NY)] + [(1, 0, s) for s in range(1, NX)]
        self.to = {
            (dz, dy, dx): (self.p, (self.zs[dz] * NY + self.ys[dy]) * NX + self.xs[dx], self.h)
            for dz, dy, dx in steps
        }

    def peers(self):
        near = [t for s, t in self.to.items() if s != (0, 0, 0)]
        across = [(self.cores[1], *self.to[step_of(axis, 0, s)][1:]) for axis in "xy" for s in RING]
        return [self.core, self.head[1], self.head[3]] + near + across


class Links:
    def __init__(self, send_sem, recv_sem):
        self.send_sem, self.recv_sem = send_sem, recv_sem
        self.count = 0

    def copy(self, number, src, dst, target):
        return pltpu.make_async_remote_copy(
            src_ref=src, dst_ref=dst, send_sem=self.send_sem.at[number],
            recv_sem=self.recv_sem.at[number], device_id=target, device_id_type=MESH,
        )

    def send(self, src, dst, target):
        number = self.count
        self.count += 1
        self.copy(number, src, dst, target).start()
        return number

    def landed(self, number, region, target):
        self.copy(number, region, region, target).wait()


def greet(peers):
    barrier = pltpu.get_barrier_semaphore()
    for peer in peers:
        pl.semaphore_signal(barrier, inc=1, device_id=peer, device_id_type=MESH)
    pl.semaphore_wait(barrier, len(peers))


def step_of(axis, dz, s):
    return (dz, s, 0) if axis == "y" else (dz, 0, s)


def along(place, axis, s):
    return (place.ys if axis == "y" else place.xs)[s]


def gather_rows(links, place, kview, vview):
    every = slice(None)
    sent = []
    for dz, s in PLANE:
        for axis, view in (("y", kview), ("x", vview)):
            own = view(place.z, place.y, place.x)
            sent.append((links.send(own, own, place.to[step_of(axis, dz, s)]), dz, s, axis, view))
    yield
    for number, dz, s, axis, view in sent:
        z, k = place.zs[dz], along(place, axis, (4 - s) % 4)
        region = view(z, k, place.x) if axis == "y" else view(z, place.y, k)
        links.landed(number, region, place.to[step_of(axis, dz, (4 - s) % 4)])
    sent = []
    for s in RING:
        for axis, view in (("x", kview), ("y", vview)):
            own = view(every, every, place.x) if axis == "x" else view(every, place.y, every)
            sent.append((links.send(own, own, place.to[step_of(axis, 0, s)]), s, axis, view))
    yield
    for number, s, axis, view in sent:
        k = along(place, axis, 4 - s)
        region = view(every, every, k) if axis == "x" else view(every, k, every)
        links.landed(number, region, place.to[step_of(axis, 0, 4 - s)])


def gather_rows_late(links, place, kview, vview):
    every = slice(None)
    partner = place.to[(1, 0, 0)]
    sent = []
    for view in (kview, vview):
        own = view(place.z, place.y, place.x)
        sent.append((links.send(own, own, partner), view))
    yield
    for number, view in sent:
        links.landed(number, view(place.zs[1], place.y, place.x), partner)
    for stage in range(2):
        sent = []
        for s in RING:
            for axis, view in (("yx"[stage], kview), ("xy"[stage], vview)):
                def region(k, axis=axis, view=view):
                    if stage == 0:
                        return view(every, k, place.x) if axis == "y" else view(every, place.y, k)
                    return view(every, k, every) if axis == "y" else view(every, every, k)
                own = region(along(place, axis, 0))
                sent.append((links.send(own, own, place.to[step_of(axis, 0, s)]), s, axis, region))
        yield
        for number, s, axis, region in sent:
            links.landed(number, region(along(place, axis, 4 - s)), place.to[step_of(axis, 0, 4 - s)])


def gather_plane(links, place, kview, vview):
    sent = []
    for dz, s in PLANE:
        for axis, view in (("y", kview), ("x", vview)):
            own = view(place.z, along(place, axis, 0))
            sent.append((links.send(own, own, place.to[step_of(axis, dz, s)]), dz, s, axis, view))
    yield
    for number, dz, s, axis, view in sent:
        back = (4 - s) % 4
        links.landed(number, view(place.zs[dz], along(place, axis, back)), place.to[step_of(axis, dz, back)])


def reduce_products(links, place, theirs, landing, done):
    sent = []
    for s in (2, 1, 3, 0):
        for core in (1, 0):
            if core or s:
                for which, axis in ((0, "x"), (1, "y")):
                    slot = 4 * core + s - 1
                    target = place.to[step_of(axis, 0, s)]
                    target = (place.cores[core], *target[1:])
                    number = links.send(theirs.at[which, core, s], landing.at[which, slot], target)
                    sent.append((number, which, axis, s, core, slot))
    yield
    for number, which, axis, s, core, slot in sent:
        target = place.to[step_of(axis, 0, (4 - s) % 4)]
        links.landed(number, landing.at[which, slot], (place.cores[core], *target[1:]))
    for which in range(2):
        total = theirs[which, 0, 0].astype(F32)
        for slot in range(7):
            total = total + landing[which, slot].astype(F32)
        done(which, total)


def reduce_rows(links, place, kterm, vterm, buf1, buf2, mid, put):
    every = slice(None)
    sent = []
    for s in RING:
        for which, axis, term in ((0, "x", kterm), (1, "y", vterm)):
            k = along(place, axis, s)
            src = term(every, every, k) if axis == "x" else term(every, k, every)
            sent.append((links.send(src, buf1.at[which, s - 1], place.to[step_of(axis, 0, s)]), which, s, axis))
    yield
    for number, which, s, axis in sent:
        links.landed(number, buf1.at[which, s - 1], place.to[step_of(axis, 0, 4 - s)])
    for which, own in ((0, kterm(every, every, place.x)), (1, vterm(every, place.y, every))):
        total = own[...].astype(F32)
        for s in range(3):
            total = total + buf1[which, s].astype(F32)
        mid[which] = total.astype(B16)
    sent = []
    for i, (dz, s) in enumerate(PLANE):
        for which, axis in ((0, "y"), (1, "x")):
            src = mid.at[which, place.zs[dz], along(place, axis, s)]
            sent.append((links.send(src, buf2.at[which, i], place.to[step_of(axis, dz, s)]), which, i, axis, dz, s))
    yield
    for number, which, i, axis, dz, s in sent:
        links.landed(number, buf2.at[which, i], place.to[step_of(axis, dz, (4 - s) % 4)])
    for which, k in ((0, place.y), (1, place.x)):
        total = mid[which, place.z, k].astype(F32)
        for i in range(len(PLANE)):
            total = total + buf2[which, i].astype(F32)
        put(which, total.astype(B16))


def swap_columns(links, place, hall, mine, turned, cols):
    half = hall.shape[1] // 2
    width = half // NZ
    partner = place.to[(1, 0, 0)]
    sent = []
    for p in range(2):
        theirs = pl.ds(pl.multiple_of(p * half + place.zs[1] * width, width), width)
        sent.append((links.send(hall.at[:, theirs], mine.at[p, place.z], partner), p))
        ours = pl.ds(pl.multiple_of(p * half + place.z * width, width), width)
        mine[p, place.z] = hall[:, ours]
    yield
    for number, p in sent:
        links.landed(number, mine.at[p, place.zs[1]], partner)
    for p in range(2):
        block = mine[p].reshape(mine.shape[1] * mine.shape[2], width)
        turned[p] = block.T.reshape(turned.shape[1:])
    sent = []
    for s in RING:
        for which, axis in ((0, "y"), (1, "x")):
            src = turned.at[:, place.ys[s]] if axis == "y" else turned.at[:, :, place.xs[s]]
            number = links.send(src, cols.at[which, along(place, axis, 0)], place.to[step_of(axis, 0, s)])
            sent.append((number, which, axis, s))
    for p in range(2):
        cols[0, place.y, p] = turned[p, place.y]
        for k in range(4):
            cols[1, place.x, p, k] = turned[p, k, place.x]
    yield
    for number, which, axis, s in sent:
        links.landed(number, cols.at[which, along(place, axis, 4 - s)], place.to[step_of(axis, 0, 4 - s)])


def layer_kernel(lengths, assign, hid, wk_hbm, wv_hbm, q_hbm, do_hbm, rk_hbm, rv_hbm,
                 o_hbm, dq_hbm, drk_hbm, drv_hbm, wk_out, wv_out,
                 hall, wk, wv, kbuf, vbuf, mine, turned, cols, lhs,
                 qb, gb, kall, vall, ob, dqb, drk, drv, dsb, erb, acck, accv, gk, gv,
                 buf1, buf2, mid, gsum, spread, theirs, landing,
                 w_sem, in_sem, out_sem, send_sem, recv_sem):
    place = Place()
    links = Links(send_sem, recv_sem)
    wide = GRP * HD

    def part(ref, b, width):
        return ref.at[b % 2, :, pl.ds((b // 2) * width, width)]

    w_loads = [pltpu.make_async_copy(s, d, w_sem.at[i]) for i, (s, d) in enumerate(((wk_hbm, wk), (wv_hbm, wv)))]
    loads = []
    for b in range(BLOCKS):
        pairs = ((part(q_hbm, b, wide), qb.at[b]), (part(do_hbm, b, wide), gb.at[b]),
                 (part(rk_hbm, b, HD), kall.at[b, pl.ds(PLEN, RLEN)]), (part(rv_hbm, b, HD), vall.at[b, pl.ds(PLEN, RLEN)]))
        loads += [pltpu.make_async_copy(s, d, in_sem.at[4 * b + i]) for i, (s, d) in enumerate(pairs)]
    for load in w_loads + loads:
        load.start()
    greet(place.peers())

    to_left, to_right = place.head[3], place.head[1]
    half = hid.shape[1] // 2
    lo, hi = pl.ds(0, half), pl.ds(half, half)
    low, high, far = (pl.ds(s, 16) for s in (16, 32, 48))
    a = links.send(hid.at[:, lo], hall.at[low, lo], to_right)
    b = links.send(hid.at[:, hi], hall.at[high, hi], to_left)
    c = links.send(hid.at[:, hi], hall.at[low, hi], to_right)
    d = links.send(hid.at[:, lo], hall.at[high, lo], to_left)
    hall[0:16] = hid[...]
    for load in w_loads:
        load.wait()

    def project(start, size):
        rows = hall[start:start + size]
        for w, out in ((wk, kbuf), (wv, vbuf)):
            block = jnp.dot(rows, w[...], preferred_element_type=F32).astype(B16)
            for g in range(2):
                out[g, place.z, place.y, place.x, start:start + size] = block[:, g * HD:(g + 1) * HD]

    def gather(how, start, size, g):
        rows = pl.ds(start, size)
        return how(
            links, place,
            lambda z, y, x: kbuf.at[g, z, y, x, rows],
            lambda z, y, x: vbuf.at[g, z, y, x, rows],
        )

    every = slice(None)
    project(0, 16)
    first = gather(gather_rows_late, 0, 16, every)
    next(first)
    links.landed(a, hall.at[low, lo], to_left)
    e = links.send(hall.at[low, lo], hall.at[far, lo], to_right)
    links.landed(b, hall.at[high, hi], to_right)
    f = links.send(hall.at[high, hi], hall.at[far, hi], to_left)
    next(first)
    links.landed(c, hall.at[low, hi], to_left)
    links.landed(d, hall.at[high, lo], to_right)
    project(16, 32)
    second = gather(gather_rows_late, 16, 32, 0)
    next(second)
    next(first)
    next(second)
    links.landed(e, hall.at[far, lo], to_left)
    links.landed(f, hall.at[far, hi], to_right)
    project(48, 16)
    third, fourth = gather(gather_rows, 48, 16, 0), gather(gather_rows, 16, 48, 1)
    next(third)
    next(fourth)
    swap = swap_columns(links, place, hall, mine, turned, cols)
    next(swap)
    next(second)
    next(third)
    for load in loads:
        load.wait()
    next(first, None)
    next(second, None)
    next(third, None)
    next(fourth)

    count = cols.shape[4]
    outs = (wk_out, wv_out)

    def chain(g):
        return run_chain(g, gsum.at[g], buf1.at[g], buf2.at[g], mid.at[g], theirs.at[g], landing.at[g])

    def run_chain(g, total, first_landing, second_landing, between, own, last_landing):
        def put(which, value):
            total[which, along(place, "yx"[which], 0), place.z] = value

        yield from reduce_rows(
            links, place,
            lambda z, y, x: gk.at[g, z, y, x],
            lambda z, y, x: gv.at[g, z, y, x],
            first_landing, second_landing, between, put,
        )
        yield from gather_plane(
            links, place,
            lambda z, y: total.at[0, y, z],
            lambda z, x: total.at[1, x, z],
        )
        for which, axis in ((0, "x"), (1, "y")):
            rhs = total[which].reshape(-1, HD)
            product = jnp.dot(lhs[which], rhs, preferred_element_type=F32).astype(B16)
            spread[g, which] = product.reshape(spread.shape[2:])
            for core in range(2):
                for s in range(4):
                    k = along(place, axis, s)
                    own[which, core, s] = spread[g, which, place.cores[core], k]

        def done(which, value):
            outs[which][:, g * HD:(g + 1) * HD] = value

        yield from reduce_products(links, place, own, last_landing, done)

    chains = [chain(0), chain(1)]
    causal = lax.broadcasted_iota(jnp.int32, (RLEN, RLEN), 1) <= lax.broadcasted_iota(jnp.int32, (RLEN, RLEN), 0)

    def block(b, _):
        g, r = b // 2, lax.rem(b, 2)

        @pl.when(b == 1)
        def _():
            next(swap)

        @pl.when(b == 2)
        def _():
            next(chains[0])
            next(fourth, None)

        is_first = assign[r] == 0
        live = lax.broadcasted_iota(jnp.int32, (RLEN, 1), 0) < lengths[r]
        for src, dst in ((kbuf, kall), (vbuf, vall)):
            dst[b, :PLEN] = jnp.where(is_first, src[g, 0].reshape(PLEN, HD), src[g, 1].reshape(PLEN, HD))
        dkt = dvt = None

        def scores(j):
            s = lax.dot_general(qb[b, :, j * HD:(j + 1) * HD], kall[b], NT, preferred_element_type=F32)
            return jnp.concatenate([s[:, :PLEN], jnp.where(causal, s[:, PLEN:], NEG_FILL)], axis=1)

        following = scores(0)
        for j in range(GRP):
            lanes = slice(j * HD, (j + 1) * HD)
            q = qb[b, :, lanes]
            v = vall[b]
            s = following
            if j + 1 < GRP:
                following = scores(j + 1)
            top = jnp.max(s, axis=1, keepdims=True)
            e = jnp.exp2((s - top) * SCALE_LOG2E)
            inv = 1.0 / jnp.sum(e, axis=1, keepdims=True)
            inv = jnp.where(live, inv, 0.0)
            e_low = e.astype(B16)
            out = (jnp.dot(e_low, v, preferred_element_type=F32) * inv).astype(B16)
            ob[b, :, lanes] = out
            grad = (gb[b, :, lanes].astype(F32) * inv).astype(B16)
            gb[b, :, lanes] = grad
            delta = jnp.sum(grad.astype(F32) * out.astype(F32), axis=1, keepdims=True)
            dp = lax.dot_general(grad, v, NT, preferred_element_type=F32)
            ds = (e * (dp - delta)).astype(B16)
            dsb[b, j] = ds
            erb[b, j] = e_low[:, PLEN:]
            kt = lax.dot_general(q, ds[:, :PLEN], TN, preferred_element_type=F32)
            vt = lax.dot_general(grad, e_low[:, :PLEN], TN, preferred_element_type=F32)
            dkt = kt if j == 0 else dkt + kt
            dvt = vt if j == 0 else dvt + vt
        dk = (dkt * SCALE).T
        dv = dvt.T

        @pl.when(r == 0)
        def _():
            for i in range(2):
                mine_too = is_first if i == 0 else jnp.logical_not(is_first)
                acck[i] = jnp.where(mine_too, dk, 0.0)
                accv[i] = jnp.where(mine_too, dv, 0.0)

        @pl.when(r == 1)
        def _():
            for i in range(2):
                mine_too = is_first if i == 0 else jnp.logical_not(is_first)
                shape = gk.shape[2:]
                gk[g, i] = (acck[i] + jnp.where(mine_too, dk, 0.0)).astype(B16).reshape(shape)
                gv[g, i] = (accv[i] + jnp.where(mine_too, dv, 0.0)).astype(B16).reshape(shape)

        return 0

    lax.fori_loop(0, BLOCKS, block, 0)

    stores = []

    def store(number, src, dst):
        copy = pltpu.make_async_copy(src, dst, out_sem.at[number])
        copy.start()
        stores.append(copy)

    def late(b):
        dkt = dvt = None
        for j in range(GRP):
            lanes = slice(j * HD, (j + 1) * HD)
            dqb[b, :, lanes] = (jnp.dot(dsb[b, j], kall[b], preferred_element_type=F32) * SCALE).astype(B16)
            kt = lax.dot_general(qb[b, :, lanes], dsb[b, j, :, PLEN:], TN, preferred_element_type=F32)
            vt = lax.dot_general(gb[b, :, lanes], erb[b, j], TN, preferred_element_type=F32)
            dkt = kt if j == 0 else dkt + kt
            dvt = vt if j == 0 else dvt + vt
        drk[b] = (dkt * SCALE).T.astype(B16)
        drv[b] = dvt.T.astype(B16)
        store(4 * b, ob.at[b], part(o_hbm, b, wide))
        store(4 * b + 1, dqb.at[b], part(dq_hbm, b, wide))
        store(4 * b + 2, drk.at[b], part(drk_hbm, b, HD))
        store(4 * b + 3, drv.at[b], part(drv_hbm, b, HD))

    next(chains[1])
    next(chains[0])
    late(0)
    late(1)
    late(2)
    next(chains[0])
    next(chains[1])
    next(swap, None)
    for which in range(2):
        for k in range(4):
            lhs[which, :, k * HD:(k + 1) * HD] = cols[which, k].reshape(lhs.shape[1], HD)
    late(3)
    next(chains[0])
    next(chains[1])
    next(chains[0], None)
    next(chains[1])
    next(chains[1], None)
    for copy in stores:
        copy.wait()


def layer(prefix_hidden, w_key, w_value, queries, resp_keys, resp_values, lengths, assign, grad_out):
    rows, depth = prefix_hidden.shape
    width = w_key.shape[1]
    count = depth // (2 * NZ * NY * NX)
    tall = 4 * rows
    S = jax.ShapeDtypeStruct
    vm = pl.BlockSpec(memory_space=pltpu.VMEM)
    sm = pl.BlockSpec(memory_space=pltpu.SMEM)
    hbm = pl.BlockSpec(memory_space=pl.ANY)
    V = pltpu.VMEM
    keys = PLEN + RLEN
    wide = GRP * HD
    copies = 192
    grads = S((count, width), F32)
    return pl.pallas_call(
        layer_kernel,
        in_specs=[sm, sm, vm] + [hbm] * 6,
        out_specs=[hbm] * 4 + [vm] * 2,
        out_shape=[S(queries.shape, B16), S(queries.shape, B16), S(resp_keys.shape, B16), S(resp_keys.shape, B16), grads, grads],
        scratch_shapes=[
            V((tall, depth), B16), V((depth, width), B16), V((depth, width), B16),
            V((2, NZ, NY, NX, tall, HD), B16), V((2, NZ, NY, NX, tall, HD), B16),
            V((2, NZ, tall, depth // 4), B16), V((2, NY, NX, count, HD), B16),
            V((2, 4, 2, 4, count, HD), B16), V((2, 8 * count, 4 * HD), B16),
            V((BLOCKS, RLEN, wide), B16), V((BLOCKS, RLEN, wide), B16),
            V((BLOCKS, keys, HD), B16), V((BLOCKS, keys, HD), B16),
            V((BLOCKS, RLEN, wide), B16), V((BLOCKS, RLEN, wide), B16),
            V((BLOCKS, RLEN, HD), B16), V((BLOCKS, RLEN, HD), B16),
            V((BLOCKS, GRP, RLEN, keys), B16), V((BLOCKS, GRP, RLEN, RLEN), B16),
            V((2, PLEN, HD), F32), V((2, PLEN, HD), F32),
            V((2, NZ, NY, NX, tall, HD), B16), V((2, NZ, NY, NX, tall, HD), B16),
            V((2, 2, 3, NZ, 4, tall, HD), B16), V((2, 2, 7, tall, HD), B16), V((2, 2, NZ, 4, tall, HD), B16),
            V((2, 2, 4, NZ, tall, HD), B16), V((2, 2, 2, 4, count, HD), B16),
            V((2, 2, 2, 4, count, HD), B16), V((2, 2, 7, count, HD), B16),
            pltpu.SemaphoreType.DMA((2,)), pltpu.SemaphoreType.DMA((4 * BLOCKS,)), pltpu.SemaphoreType.DMA((4 * BLOCKS,)),
            pltpu.SemaphoreType.DMA((copies,)), pltpu.SemaphoreType.DMA((copies,)),
        ],
        compiler_params=pltpu.CompilerParams(collective_id=0, has_side_effects=True, vmem_limit_bytes=VMEM_LIMIT),
        name="layer",
    )(lengths, assign, prefix_hidden, w_key, w_value, queries, grad_out, resp_keys, resp_values)


def hand_over_kernel(*refs):
    count = (len(refs) - 2) // 3
    sources, targets, held = refs[:count], refs[count:2 * count], refs[2 * count:3 * count]
    in_sem, out_sem = refs[3 * count:]
    reads, writes = [], []
    for i in range(count):
        for part in range(2):
            rows = pl.ds(part * (sources[i].shape[0] // 2), sources[i].shape[0] // 2)
            number = 2 * i + part
            reads.append(pltpu.make_async_copy(sources[i].at[rows], held[i].at[rows], in_sem.at[number]))
            writes.append(pltpu.make_async_copy(held[i].at[rows], targets[i].at[rows], out_sem.at[number]))
    for copy in reads:
        copy.start()
    for read, write in zip(reads, writes):
        read.wait()
        write.start()
    for copy in writes:
        copy.wait()


def hand_over(*arrays):
    hbm = pl.BlockSpec(memory_space=pl.ANY)
    return pl.pallas_call(
        hand_over_kernel,
        in_specs=[hbm] * len(arrays),
        out_specs=[hbm] * len(arrays),
        out_shape=[jax.ShapeDtypeStruct(a.shape, a.dtype) for a in arrays],
        scratch_shapes=[pltpu.VMEM(a.shape, a.dtype) for a in arrays]
        + [pltpu.SemaphoreType.DMA((2 * len(arrays),)), pltpu.SemaphoreType.DMA((2 * len(arrays),))],
        name="hand_over",
    )(*arrays)


def body(*arrays):
    return tuple(hand_over(*layer(*arrays)))


def solution(mesh):
    return jax.shard_map(
        body,
        mesh=mesh,
        in_specs=(
            P(("prompt", "resp", "head"), None),
            P(None, "head"),
            P(None, "head"),
            P(("prompt", "resp"), None, "head"),
            P(("prompt", "resp"), None, "head"),
            P(("prompt", "resp"), None, "head"),
            P(("prompt", "resp")),
            P(("prompt", "resp")),
            P(("prompt", "resp"), None, "head"),
        ),
        out_specs=(
            P(("prompt", "resp"), None, "head"),
            P(("prompt", "resp"), None, "head"),
            P(("prompt", "resp"), None, "head"),
            P(("prompt", "resp"), None, "head"),
            P(("prompt", "resp"), "head"),
            P(("prompt", "resp"), "head"),
        ),
        check_vma=False,
    )
```

```python
import math

import jax
import jax.numpy as jnp
from jax import lax
from jax.experimental import pallas as pl
from jax.experimental.pallas import tpu as pltpu
from jax.sharding import PartitionSpec as P

HD = 128
PLEN = 1024
RLEN = 256
GRP = 5
NX = NY = 4
NZ = 2
NEG_FILL = -1e30
SCALE = 1.0 / math.sqrt(HD)
SCALE_LOG2E = SCALE * math.log2(math.e)
NT = (((1,), (1,)), ((), ()))
TN = (((0,), (0,)), ((), ()))
MESH = pl.DeviceIdType.MESH
F32 = jnp.float32
B16 = jnp.bfloat16
VMEM_LIMIT = 56 * 2**20


PLANE = ((0, 1), (0, 3), (1, 0), (1, 1), (1, 3), (0, 2), (1, 2))
RING = (1, 3, 2)
BLOCKS = 4


class Place:
    def __init__(self):
        self.p = lax.axis_index("prompt")
        self.r = lax.axis_index("resp")
        self.h = lax.axis_index("head")
        self.z = self.r // (NY * NX)
        self.y = lax.rem(self.r // NX, NY)
        self.x = lax.rem(self.r, NX)
        self.zs = [self.z, 1 - self.z]
        self.ys = [lax.rem(self.y + s, NY) for s in range(NY)]
        self.xs = [lax.rem(self.x + s, NX) for s in range(NX)]
        self.cores = [self.p, 1 - self.p]
        self.core = (1 - self.p, self.r, self.h)
        self.head = [(self.p, self.r, lax.rem(self.h + s, 4)) for s in range(4)]
        steps = [(0, s, 0) for s in range(NY)] + [(0, 0, s) for s in range(1, NX)]
        steps += [(1, s, 0) for s in range(NY)] + [(1, 0, s) for s in range(1, NX)]
        self.to = {
            (dz, dy, dx): (self.p, (self.zs[dz] * NY + self.ys[dy]) * NX + self.xs[dx], self.h)
            for dz, dy, dx in steps
        }

    def peers(self):
        near = [t for s, t in self.to.items() if s != (0, 0, 0)]
        across = [(self.cores[1], *self.to[step_of(axis, 0, s)][1:]) for axis in "xy" for s in RING]
        return [self.core, self.head[1], self.head[3]] + near + across


class Links:
    def __init__(self, send_sem, recv_sem):
        self.send_sem, self.recv_sem = send_sem, recv_sem
        self.count = 0

    def copy(self, number, src, dst, target):
        return pltpu.make_async_remote_copy(
            src_ref=src, dst_ref=dst, send_sem=self.send_sem.at[number],
            recv_sem=self.recv_sem.at[number], device_id=target, device_id_type=MESH,
        )

    def send(self, src, dst, target):
        number = self.count
        self.count += 1
        self.copy(number, src, dst, target).start()
        return number

    def landed(self, number, region, target):
        self.copy(number, region, region, target).wait()


def greet(peers):
    barrier = pltpu.get_barrier_semaphore()
    for peer in peers:
        pl.semaphore_signal(barrier, inc=1, device_id=peer, device_id_type=MESH)
    pl.semaphore_wait(barrier, len(peers))


def step_of(axis, dz, s):
    return (dz, s, 0) if axis == "y" else (dz, 0, s)


def along(place, axis, s):
    return (place.ys if axis == "y" else place.xs)[s]


def gather_rows(links, place, kview, vview):
    every = slice(None)
    sent = []
    for dz, s in PLANE:
        for axis, view in (("y", kview), ("x", vview)):
            own = view(place.z, place.y, place.x)
            sent.append((links.send(own, own, place.to[step_of(axis, dz, s)]), dz, s, axis, view))
    yield
    for number, dz, s, axis, view in sent:
        z, k = place.zs[dz], along(place, axis, (4 - s) % 4)
        region = view(z, k, place.x) if axis == "y" else view(z, place.y, k)
        links.landed(number, region, place.to[step_of(axis, dz, (4 - s) % 4)])
    sent = []
    for s in RING:
        for axis, view in (("x", kview), ("y", vview)):
            own = view(every, every, place.x) if axis == "x" else view(every, place.y, every)
            sent.append((links.send(own, own, place.to[step_of(axis, 0, s)]), s, axis, view))
    yield
    for number, s, axis, view in sent:
        k = along(place, axis, 4 - s)
        region = view(every, every, k) if axis == "x" else view(every, k, every)
        links.landed(number, region, place.to[step_of(axis, 0, 4 - s)])


def gather_rows_late(links, place, kview, vview):
    every = slice(None)
    partner = place.to[(1, 0, 0)]
    sent = []
    for view in (kview, vview):
        own = view(place.z, place.y, place.x)
        sent.append((links.send(own, own, partner), view))
    yield
    for number, view in sent:
        links.landed(number, view(place.zs[1], place.y, place.x), partner)
    for stage in range(2):
        sent = []
        for s in RING:
            for axis, view in (("yx"[stage], kview), ("xy"[stage], vview)):
                def region(k, axis=axis, view=view):
                    if stage == 0:
                        return view(every, k, place.x) if axis == "y" else view(every, place.y, k)
                    return view(every, k, every) if axis == "y" else view(every, every, k)
                own = region(along(place, axis, 0))
                sent.append((links.send(own, own, place.to[step_of(axis, 0, s)]), s, axis, region))
        yield
        for number, s, axis, region in sent:
            links.landed(number, region(along(place, axis, 4 - s)), place.to[step_of(axis, 0, 4 - s)])


def gather_plane(links, place, kview, vview):
    sent = []
    for dz, s in PLANE:
        for axis, view in (("y", kview), ("x", vview)):
            own = view(place.z, along(place, axis, 0))
            sent.append((links.send(own, own, place.to[step_of(axis, dz, s)]), dz, s, axis, view))
    yield
    for number, dz, s, axis, view in sent:
        back = (4 - s) % 4
        links.landed(number, view(place.zs[dz], along(place, axis, back)), place.to[step_of(axis, dz, back)])


def reduce_products(links, place, theirs, landing, done):
    sent = []
    for s in (2, 1, 3, 0):
        for core in (1, 0):
            if core or s:
                for which, axis in ((0, "x"), (1, "y")):
                    slot = 4 * core + s - 1
                    target = place.to[step_of(axis, 0, s)]
                    target = (place.cores[core], *target[1:])
                    number = links.send(theirs.at[which, core, s], landing.at[which, slot], target)
                    sent.append((number, which, axis, s, core, slot))
    yield
    for number, which, axis, s, core, slot in sent:
        target = place.to[step_of(axis, 0, (4 - s) % 4)]
        links.landed(number, landing.at[which, slot], (place.cores[core], *target[1:]))
    for which in range(2):
        total = theirs[which, 0, 0].astype(F32)
        for slot in range(7):
            total = total + landing[which, slot].astype(F32)
        done(which, total)


def reduce_rows(links, place, kterm, vterm, buf1, buf2, mid, put):
    every = slice(None)
    sent = []
    for s in RING:
        for which, axis, term in ((0, "x", kterm), (1, "y", vterm)):
            k = along(place, axis, s)
            src = term(every, every, k) if axis == "x" else term(every, k, every)
            sent.append((links.send(src, buf1.at[which, s - 1], place.to[step_of(axis, 0, s)]), which, s, axis))
    yield
    for number, which, s, axis in sent:
        links.landed(number, buf1.at[which, s - 1], place.to[step_of(axis, 0, 4 - s)])
    for which, own in ((0, kterm(every, every, place.x)), (1, vterm(every, place.y, every))):
        total = own[...].astype(F32)
        for s in range(3):
            total = total + buf1[which, s].astype(F32)
        mid[which] = total.astype(B16)
    sent = []
    for i, (dz, s) in enumerate(PLANE):
        for which, axis in ((0, "y"), (1, "x")):
            src = mid.at[which, place.zs[dz], along(place, axis, s)]
            sent.append((links.send(src, buf2.at[which, i], place.to[step_of(axis, dz, s)]), which, i, axis, dz, s))
    yield
    for number, which, i, axis, dz, s in sent:
        links.landed(number, buf2.at[which, i], place.to[step_of(axis, dz, (4 - s) % 4)])
    for which, k in ((0, place.y), (1, place.x)):
        total = mid[which, place.z, k].astype(F32)
        for i in range(len(PLANE)):
            total = total + buf2[which, i].astype(F32)
        put(which, total.astype(B16))


def swap_columns(links, place, hall, mine, turned, cols):
    half = hall.shape[1] // 2
    width = half // NZ
    partner = place.to[(1, 0, 0)]
    sent = []
    for p in range(2):
        theirs = pl.ds(pl.multiple_of(p * half + place.zs[1] * width, width), width)
        sent.append((links.send(hall.at[:, theirs], mine.at[p, place.z], partner), p))
        ours = pl.ds(pl.multiple_of(p * half + place.z * width, width), width)
        mine[p, place.z] = hall[:, ours]
    yield
    for number, p in sent:
        links.landed(number, mine.at[p, place.zs[1]], partner)
    for p in range(2):
        block = mine[p].reshape(mine.shape[1] * mine.shape[2], width)
        turned[p] = block.T.reshape(turned.shape[1:])
    sent = []
    for s in RING:
        for which, axis in ((0, "y"), (1, "x")):
            src = turned.at[:, place.ys[s]] if axis == "y" else turned.at[:, :, place.xs[s]]
            number = links.send(src, cols.at[which, along(place, axis, 0)], place.to[step_of(axis, 0, s)])
            sent.append((number, which, axis, s))
    for p in range(2):
        cols[0, place.y, p] = turned[p, place.y]
        for k in range(4):
            cols[1, place.x, p, k] = turned[p, k, place.x]
    yield
    for number, which, axis, s in sent:
        links.landed(number, cols.at[which, along(place, axis, 4 - s)], place.to[step_of(axis, 0, 4 - s)])


def layer_kernel(lengths, assign, hid, wk_hbm, wv_hbm, q_hbm, do_hbm, rk_hbm, rv_hbm,
                 o_hbm, dq_hbm, drk_hbm, drv_hbm, wk_out, wv_out,
                 hall, wk, wv, kbuf, vbuf, mine, turned, cols, lhs,
                 qb, gb, kall, vall, ob, dqb, drk, drv, dsb, erb, acck, accv, gk, gv,
                 buf1, buf2, mid, gsum, spread, theirs, landing,
                 w_sem, in_sem, out_sem, send_sem, recv_sem):
    place = Place()
    links = Links(send_sem, recv_sem)
    wide = GRP * HD

    def part(ref, b, width):
        return ref.at[b % 2, :, pl.ds((b // 2) * width, width)]

    w_loads = [pltpu.make_async_copy(s, d, w_sem.at[i]) for i, (s, d) in enumerate(((wk_hbm, wk), (wv_hbm, wv)))]
    loads = []
    for b in range(BLOCKS):
        pairs = ((part(q_hbm, b, wide), qb.at[b]), (part(do_hbm, b, wide), gb.at[b]),
                 (part(rk_hbm, b, HD), kall.at[b, pl.ds(PLEN, RLEN)]), (part(rv_hbm, b, HD), vall.at[b, pl.ds(PLEN, RLEN)]))
        loads += [pltpu.make_async_copy(s, d, in_sem.at[4 * b + i]) for i, (s, d) in enumerate(pairs)]
    for load in w_loads + loads:
        load.start()
    greet(place.peers())

    to_left, to_right = place.head[3], place.head[1]
    half = hid.shape[1] // 2
    lo, hi = pl.ds(0, half), pl.ds(half, half)
    low, high, far = (pl.ds(s, 16) for s in (16, 32, 48))
    a = links.send(hid.at[:, lo], hall.at[low, lo], to_right)
    b = links.send(hid.at[:, hi], hall.at[high, hi], to_left)
    c = links.send(hid.at[:, hi], hall.at[low, hi], to_right)
    d = links.send(hid.at[:, lo], hall.at[high, lo], to_left)
    hall[0:16] = hid[...]
    for load in w_loads:
        load.wait()

    def project(start, size):
        rows = hall[start:start + size]
        for w, out in ((wk, kbuf), (wv, vbuf)):
            block = jnp.dot(rows, w[...], preferred_element_type=F32).astype(B16)
            for g in range(2):
                out[g, place.z, place.y, place.x, start:start + size] = block[:, g * HD:(g + 1) * HD]

    def gather(how, start, size, g):
        rows = pl.ds(start, size)
        return how(
            links, place,
            lambda z, y, x: kbuf.at[g, z, y, x, rows],
            lambda z, y, x: vbuf.at[g, z, y, x, rows],
        )

    every = slice(None)
    project(0, 16)
    first = gather(gather_rows_late, 0, 16, every)
    next(first)
    links.landed(a, hall.at[low, lo], to_left)
    e = links.send(hall.at[low, lo], hall.at[far, lo], to_right)
    links.landed(b, hall.at[high, hi], to_right)
    f = links.send(hall.at[high, hi], hall.at[far, hi], to_left)
    next(first)
    links.landed(c, hall.at[low, hi], to_left)
    links.landed(d, hall.at[high, lo], to_right)
    project(16, 32)
    second = gather(gather_rows_late, 16, 32, 0)
    next(second)
    next(first)
    next(second)
    links.landed(e, hall.at[far, lo], to_left)
    links.landed(f, hall.at[far, hi], to_right)
    project(48, 16)
    third, fourth = gather(gather_rows, 48, 16, 0), gather(gather_rows, 16, 48, 1)
    next(third)
    next(fourth)
    swap = swap_columns(links, place, hall, mine, turned, cols)
    next(swap)
    next(second)
    next(third)
    for load in loads:
        load.wait()
    next(first, None)
    next(second, None)
    next(third, None)
    next(fourth)

    count = cols.shape[4]
    outs = (wk_out, wv_out)

    def chain(g):
        return run_chain(g, gsum.at[g], buf1.at[g], buf2.at[g], mid.at[g], theirs.at[g], landing.at[g])

    def run_chain(g, total, first_landing, second_landing, between, own, last_landing):
        def put(which, value):
            total[which, along(place, "yx"[which], 0), place.z] = value

        yield from reduce_rows(
            links, place,
            lambda z, y, x: gk.at[g, z, y, x],
            lambda z, y, x: gv.at[g, z, y, x],
            first_landing, second_landing, between, put,
        )
        yield from gather_plane(
            links, place,
            lambda z, y: total.at[0, y, z],
            lambda z, x: total.at[1, x, z],
        )
        for which, axis in ((0, "x"), (1, "y")):
            rhs = total[which].reshape(-1, HD)
            product = jnp.dot(lhs[which], rhs, preferred_element_type=F32).astype(B16)
            spread[g, which] = product.reshape(spread.shape[2:])
            for core in range(2):
                for s in range(4):
                    k = along(place, axis, s)
                    own[which, core, s] = spread[g, which, place.cores[core], k]

        def done(which, value):
            outs[which][:, g * HD:(g + 1) * HD] = value

        yield from reduce_products(links, place, own, last_landing, done)

    chains = [chain(0), chain(1)]
    causal = lax.broadcasted_iota(jnp.int32, (RLEN, RLEN), 1) <= lax.broadcasted_iota(jnp.int32, (RLEN, RLEN), 0)

    def block(b, _):
        g, r = b // 2, lax.rem(b, 2)

        @pl.when(b == 1)
        def _():
            next(swap)

        @pl.when(b == 2)
        def _():
            next(chains[0])
            next(fourth, None)

        is_first = assign[r] == 0
        live = lax.broadcasted_iota(jnp.int32, (RLEN, 1), 0) < lengths[r]
        for src, dst in ((kbuf, kall), (vbuf, vall)):
            dst[b, :PLEN] = jnp.where(is_first, src[g, 0].reshape(PLEN, HD), src[g, 1].reshape(PLEN, HD))
        dkt = dvt = None

        def scores(j):
            s = lax.dot_general(qb[b, :, j * HD:(j + 1) * HD], kall[b], NT, preferred_element_type=F32)
            return jnp.concatenate([s[:, :PLEN], jnp.where(causal, s[:, PLEN:], NEG_FILL)], axis=1)

        following = scores(0)
        for j in range(GRP):
            lanes = slice(j * HD, (j + 1) * HD)
            q = qb[b, :, lanes]
            v = vall[b]
            s = following
            if j + 1 < GRP:
                following = scores(j + 1)
            top = jnp.max(s, axis=1, keepdims=True)
            e = jnp.exp2((s - top) * SCALE_LOG2E)
            inv = 1.0 / jnp.sum(e, axis=1, keepdims=True)
            inv = jnp.where(live, inv, 0.0)
            e_low = e.astype(B16)
            out = (jnp.dot(e_low, v, preferred_element_type=F32) * inv).astype(B16)
            ob[b, :, lanes] = out
            grad = (gb[b, :, lanes].astype(F32) * inv).astype(B16)
            gb[b, :, lanes] = grad
            delta = jnp.sum(grad.astype(F32) * out.astype(F32), axis=1, keepdims=True)
            dp = lax.dot_general(grad, v, NT, preferred_element_type=F32)
            ds = (e * (dp - delta)).astype(B16)
            dsb[b, j] = ds
            erb[b, j] = e_low[:, PLEN:]
            kt = lax.dot_general(q, ds[:, :PLEN], TN, preferred_element_type=F32)
            vt = lax.dot_general(grad, e_low[:, :PLEN], TN, preferred_element_type=F32)
            dkt = kt if j == 0 else dkt + kt
            dvt = vt if j == 0 else dvt + vt
            if j == 3:
                @pl.when(b == 3)
                def _():
                    next(chains[0])
        dk = (dkt * SCALE).T
        dv = dvt.T

        @pl.when(r == 0)
        def _():
            for i in range(2):
                mine_too = is_first if i == 0 else jnp.logical_not(is_first)
                acck[i] = jnp.where(mine_too, dk, 0.0)
                accv[i] = jnp.where(mine_too, dv, 0.0)

        @pl.when(r == 1)
        def _():
            for i in range(2):
                mine_too = is_first if i == 0 else jnp.logical_not(is_first)
                shape = gk.shape[2:]
                gk[g, i] = (acck[i] + jnp.where(mine_too, dk, 0.0)).astype(B16).reshape(shape)
                gv[g, i] = (accv[i] + jnp.where(mine_too, dv, 0.0)).astype(B16).reshape(shape)

        return 0

    lax.fori_loop(0, BLOCKS, block, 0)

    stores = []

    def store(number, src, dst):
        copy = pltpu.make_async_copy(src, dst, out_sem.at[number])
        copy.start()
        stores.append(copy)

    def late(b):
        dkt = dvt = None
        for j in range(GRP):
            lanes = slice(j * HD, (j + 1) * HD)
            dqb[b, :, lanes] = (jnp.dot(dsb[b, j], kall[b], preferred_element_type=F32) * SCALE).astype(B16)
            kt = lax.dot_general(qb[b, :, lanes], dsb[b, j, :, PLEN:], TN, preferred_element_type=F32)
            vt = lax.dot_general(gb[b, :, lanes], erb[b, j], TN, preferred_element_type=F32)
            dkt = kt if j == 0 else dkt + kt
            dvt = vt if j == 0 else dvt + vt
        drk[b] = (dkt * SCALE).T.astype(B16)
        drv[b] = dvt.T.astype(B16)
        store(4 * b, ob.at[b], part(o_hbm, b, wide))
        store(4 * b + 1, dqb.at[b], part(dq_hbm, b, wide))
        store(4 * b + 2, drk.at[b], part(drk_hbm, b, HD))
        store(4 * b + 3, drv.at[b], part(drv_hbm, b, HD))

    next(chains[1])
    late(0)
    next(chains[0])
    late(1)
    late(2)
    next(chains[1])
    next(swap, None)
    for which in range(2):
        for k in range(4):
            lhs[which, :, k * HD:(k + 1) * HD] = cols[which, k].reshape(lhs.shape[1], HD)
    late(3)
    next(chains[0])
    next(chains[1])
    next(chains[0], None)
    next(chains[1])
    next(chains[1], None)
    for copy in stores:
        copy.wait()


def layer(prefix_hidden, w_key, w_value, queries, resp_keys, resp_values, lengths, assign, grad_out):
    rows, depth = prefix_hidden.shape
    width = w_key.shape[1]
    count = depth // (2 * NZ * NY * NX)
    tall = 4 * rows
    S = jax.ShapeDtypeStruct
    vm = pl.BlockSpec(memory_space=pltpu.VMEM)
    sm = pl.BlockSpec(memory_space=pltpu.SMEM)
    hbm = pl.BlockSpec(memory_space=pl.ANY)
    V = pltpu.VMEM
    keys = PLEN + RLEN
    wide = GRP * HD
    copies = 192
    grads = S((count, width), F32)
    return pl.pallas_call(
        layer_kernel,
        in_specs=[sm, sm, vm] + [hbm] * 6,
        out_specs=[hbm] * 4 + [vm] * 2,
        out_shape=[S(queries.shape, B16), S(queries.shape, B16), S(resp_keys.shape, B16), S(resp_keys.shape, B16), grads, grads],
        scratch_shapes=[
            V((tall, depth), B16), V((depth, width), B16), V((depth, width), B16),
            V((2, NZ, NY, NX, tall, HD), B16), V((2, NZ, NY, NX, tall, HD), B16),
            V((2, NZ, tall, depth // 4), B16), V((2, NY, NX, count, HD), B16),
            V((2, 4, 2, 4, count, HD), B16), V((2, 8 * count, 4 * HD), B16),
            V((BLOCKS, RLEN, wide), B16), V((BLOCKS, RLEN, wide), B16),
            V((BLOCKS, keys, HD), B16), V((BLOCKS, keys, HD), B16),
            V((BLOCKS, RLEN, wide), B16), V((BLOCKS, RLEN, wide), B16),
            V((BLOCKS, RLEN, HD), B16), V((BLOCKS, RLEN, HD), B16),
            V((BLOCKS, GRP, RLEN, keys), B16), V((BLOCKS, GRP, RLEN, RLEN), B16),
            V((2, PLEN, HD), F32), V((2, PLEN, HD), F32),
            V((2, NZ, NY, NX, tall, HD), B16), V((2, NZ, NY, NX, tall, HD), B16),
            V((2, 2, 3, NZ, 4, tall, HD), B16), V((2, 2, 7, tall, HD), B16), V((2, 2, NZ, 4, tall, HD), B16),
            V((2, 2, 4, NZ, tall, HD), B16), V((2, 2, 2, 4, count, HD), B16),
            V((2, 2, 2, 4, count, HD), B16), V((2, 2, 7, count, HD), B16),
            pltpu.SemaphoreType.DMA((2,)), pltpu.SemaphoreType.DMA((4 * BLOCKS,)), pltpu.SemaphoreType.DMA((4 * BLOCKS,)),
            pltpu.SemaphoreType.DMA((copies,)), pltpu.SemaphoreType.DMA((copies,)),
        ],
        compiler_params=pltpu.CompilerParams(collective_id=0, has_side_effects=True, vmem_limit_bytes=VMEM_LIMIT),
        name="layer",
    )(lengths, assign, prefix_hidden, w_key, w_value, queries, grad_out, resp_keys, resp_values)


def hand_over_kernel(*refs):
    count = (len(refs) - 2) // 3
    sources, targets, held = refs[:count], refs[count:2 * count], refs[2 * count:3 * count]
    in_sem, out_sem = refs[3 * count:]
    reads, writes = [], []
    for i in range(count):
        for part in range(2):
            rows = pl.ds(part * (sources[i].shape[0] // 2), sources[i].shape[0] // 2)
            number = 2 * i + part
            reads.append(pltpu.make_async_copy(sources[i].at[rows], held[i].at[rows], in_sem.at[number]))
            writes.append(pltpu.make_async_copy(held[i].at[rows], targets[i].at[rows], out_sem.at[number]))
    for copy in reads:
        copy.start()
    for read, write in zip(reads, writes):
        read.wait()
        write.start()
    for copy in writes:
        copy.wait()


def hand_over(*arrays):
    hbm = pl.BlockSpec(memory_space=pl.ANY)
    return pl.pallas_call(
        hand_over_kernel,
        in_specs=[hbm] * len(arrays),
        out_specs=[hbm] * len(arrays),
        out_shape=[jax.ShapeDtypeStruct(a.shape, a.dtype) for a in arrays],
        scratch_shapes=[pltpu.VMEM(a.shape, a.dtype) for a in arrays]
        + [pltpu.SemaphoreType.DMA((2 * len(arrays),)), pltpu.SemaphoreType.DMA((2 * len(arrays),))],
        name="hand_over",
    )(*arrays)


def body(*arrays):
    return tuple(hand_over(*layer(*arrays)))


def solution(mesh):
    return jax.shard_map(
        body,
        mesh=mesh,
        in_specs=(
            P(("prompt", "resp", "head"), None),
            P(None, "head"),
            P(None, "head"),
            P(("prompt", "resp"), None, "head"),
            P(("prompt", "resp"), None, "head"),
            P(("prompt", "resp"), None, "head"),
            P(("prompt", "resp")),
            P(("prompt", "resp")),
            P(("prompt", "resp"), None, "head"),
        ),
        out_specs=(
            P(("prompt", "resp"), None, "head"),
            P(("prompt", "resp"), None, "head"),
            P(("prompt", "resp"), None, "head"),
            P(("prompt", "resp"), None, "head"),
            P(("prompt", "resp"), "head"),
            P(("prompt", "resp"), "head"),
        ),
        check_vma=False,
    )
```
